256 devices in a mesh: ta: 4 (over z_lo), gx: 8 (over y, z_hi), gy: 8 (over x, core).
Axes of the slice: x: 4, y: 4, z: 8 (z_hi: 2, z_lo: 4; z = z_hi * 4 + z_lo), core: 2. Of those that a mesh axis runs over, the one named last changes fastest.
Arguments:
- momenta: float32 [3, 128, 512, 1024], P(None, 'ta', 'gx', 'gy'), may hold values from -3 to 4.1, as said below
- potential: float32 [128, 512, 1024], P('ta', 'gx', 'gy'), may hold values from -6 to 6
- rho_start: float32 [512, 1024], P('gx', 'gy'), may hold values from 0.25 to 4
- rho_end: float32 [512, 1024], P('gx', 'gy'), may hold values from 0.25 to 4
Outputs:
- updated_momenta: float32 [3, 128, 512, 1024], P(None, 'ta', 'gx', 'gy')
- updated_potential: float32 [128, 512, 1024], P('ta', 'gx', 'gy')
The draws below stay inside these ranges and needn't reach their ends.
Inputs may be any that keep to these rules, and one draw needn't show every extreme that they name: `momenta`: component 0 (density) is positive, between 0.22 and 4.1; components 1 and 2 lie between -3 and 3.
All inputs are finite; a program needn't handle non-finite values.
Results may differ from the reference program's by a relative error of at most 0.0007.
Values sent between devices are 32-bit elements; how exact they have to be, the bound alone decides.
A program may use at most 128 MiB of HBM per device.

```python
import math
import jax
import jax.numpy as jnp
from jax import lax

NT = 128
NX = 512
NY = 1024
ITERS = 2
NEWTON = 8


def draw_momenta(key, part):
    key = jax.random.fold_in(key, 7)
    key_density, key_flux = jax.random.split(key)
    density = jnp.exp(jax.random.uniform(key_density, (1, NT, NX, NY), minval=-1.5, maxval=1.0))
    flux = jnp.clip(0.8 * jax.random.normal(key_flux, (2, NT, NX, NY)), -3.0, 3.0)
    return jnp.concatenate([density, flux], axis=0).astype(jnp.float32)


def level_of(stream_key, extent, cuts, smallest, high):
    loudness = 1.0
    for position, parts in cuts:
        draws = jax.random.uniform(jax.random.fold_in(jax.random.fold_in(stream_key, 6), position), (parts,), jnp.float32, smallest / len(cuts), high / len(cuts))
        loudness = loudness * jnp.repeat(jnp.exp(draws), extent[position] // parts).reshape((-1,) + (1,) * (len(extent) - 1 - position))
    return loudness


def bell_draw(rng, extent, width, reach, cuts=(), held_as=jnp.bfloat16):
    level = level_of(rng, extent, cuts, -0.22, 0.18) if cuts else 1.0
    array = jax.random.normal(rng, extent, jnp.float32) * width * level
    return jnp.minimum(jnp.maximum(array, -reach), reach).astype(held_as)


def setup_inputs(seed: int = 0) -> dict:
    splits = jax.random.split(jax.random.key(seed), 5)
    return {
        "momenta": draw_momenta(jax.random.fold_in(splits[4], 71), 0),
        "potential": bell_draw(splits[1], (NT, NX, NY), 1.0, 6.0, ((0, 4), (1, 8), (2, 8)), jnp.float32),
        "rho_start": jnp.clip(jnp.exp(math.log(4.0) - 2.7725887 * jax.random.uniform(splits[2], (NX, NY), jnp.float32) ** level_of(splits[2], (NX, NY), ((0, 8), (1, 8)), -0.2, 0.2)), 0.25, 4.0),
        "rho_end": jnp.clip(jnp.exp(math.log(4.0) - 2.7725887 * jax.random.uniform(splits[3], (NX, NY), jnp.float32) ** level_of(splits[3], (NX, NY), ((0, 8), (1, 8)), -0.2, 0.2)), 0.25, 4.0),
    }


penalty = 1.0
highest = lax.Precision.HIGHEST

def cosine_table(count):
    modes = jnp.arange(count, dtype=jnp.int32)[:, None]
    cells = jnp.arange(count, dtype=jnp.int32)[None, :]
    phase = modes * (2 * cells + 1) % (4 * count)
    angle = phase.astype(jnp.float32) * (jnp.pi / (2 * count))
    weight = jnp.where(modes == 0, 1.0, 2.0).astype(jnp.float32) / count
    return jnp.sqrt(weight) * jnp.cos(angle)

def eigenvalue(modes, count):
    half_angle = modes.astype(jnp.float32) * (jnp.pi / (2 * count))
    return (2.0 * jnp.sin(half_angle)) ** 2

def multiplier(time_modes, x_modes, y_modes):
    spectrum = eigenvalue(time_modes, NT)[:, None, None] + eigenvalue(x_modes, NX)[None, :, None] + eigenvalue(y_modes, NY)[None, None, :]
    anchor = ((time_modes[:, None, None] == 0) & (x_modes[None, :, None] == 0) & (y_modes[None, None, :] == 0)).astype(jnp.float32)
    return (1.0 - anchor) / (penalty * (spectrum + anchor))

def project(lifted):
    along_time, along_x, along_y = (lifted[0], lifted[1], lifted[2])
    squares = along_x * along_x + along_y * along_y
    shift_value = jnp.zeros_like(along_time)
    for newton_index in range(NEWTON):
        growth = 1.0 + shift_value
        residual = along_time - shift_value + squares / (2.0 * growth * growth)
        slope = -1.0 - squares / (growth * growth * growth)
        shift_value = jnp.maximum(shift_value - residual / slope, 0.0)
    growth = 1.0 + shift_value
    return jnp.stack([along_time - shift_value, along_x / growth, along_y / growth])

def transform(field, tables, inverse):
    for axis_index in range(3):
        table = tables[axis_index].T if inverse else tables[axis_index]
        moved = jnp.tensordot(table, field, axes=((1,), (axis_index,)), precision=highest)
        field = jnp.moveaxis(moved, 0, axis_index)
    return field

def reference(momenta, potential, rho_start, rho_end):
    time_cells = jnp.arange(NT, dtype=jnp.int32)
    x_cells = jnp.arange(NX, dtype=jnp.int32)
    y_cells = jnp.arange(NY, dtype=jnp.int32)
    keep_time = (time_cells < NT - 1).astype(jnp.float32)[:, None, None]
    keep_x = (x_cells < NX - 1).astype(jnp.float32)[None, :, None]
    keep_y = (y_cells < NY - 1).astype(jnp.float32)[None, None, :]
    first_plane = (time_cells == 0).astype(jnp.float32)[:, None, None]
    last_plane = (time_cells == NT - 1).astype(jnp.float32)[:, None, None]
    boundary = last_plane * rho_end[None] - first_plane * rho_start[None]
    tables = (cosine_table(NT), cosine_table(NX), cosine_table(NY))
    spectral_scale = multiplier(time_cells, x_cells, y_cells)
    widths = ((0, 0), (1, 1), (1, 1), (1, 1))
    for sweep_index in range(ITERS):
        padded = jnp.pad(potential[None], widths)
        slopes = jnp.stack([(padded[0, 2:, 1:-1, 1:-1] - potential) * keep_time, (padded[0, 1:-1, 2:, 1:-1] - potential) * keep_x, (padded[0, 1:-1, 1:-1, 2:] - potential) * keep_y])
        lifted = slopes + momenta / penalty
        cone = project(lifted)
        momenta = momenta + penalty * (slopes - cone)
        flows = momenta - penalty * cone
        masked = jnp.stack([flows[0] * keep_time, flows[1] * keep_x, flows[2] * keep_y])
        padded = jnp.pad(masked, widths)
        source = masked[0] - padded[0, :-2, 1:-1, 1:-1] + (masked[1] - padded[1, 1:-1, :-2, 1:-1]) + (masked[2] - padded[2, 1:-1, 1:-1, :-2]) + boundary
        spectral = transform(source, tables, False) * spectral_scale
        potential = transform(spectral, tables, True)
    return (momenta, potential)
```

```python
import functools

import jax
import jax.numpy as jnp
import numpy as np
from jax import lax
from jax.experimental import pallas as pl
from jax.experimental.pallas import tpu as pltpu
from jax.sharding import PartitionSpec as P

NT = 128
NX = 512
NY = 1024
ITERS = 2
NEWTON = 8
ROWS = 8

MESH = pl.DeviceIdType.MESH


def cosine_table(count):
    modes = np.arange(count, dtype=np.int64)[:, None]
    cells = np.arange(count, dtype=np.int64)[None, :]
    phase = modes * (2 * cells + 1) % (4 * count)
    weight = np.where(modes == 0, 1.0, 2.0) / count
    return np.sqrt(weight) * np.cos(phase * (np.pi / (2 * count)))


def eigenvalue(count):
    return (2.0 * np.sin(np.arange(count) * (np.pi / (2 * count)))) ** 2


def matmul(left, right):
    return jnp.dot(
        left, right, precision=lax.Precision.HIGHEST, preferred_element_type=jnp.float32
    )


def middle(ref, index):
    rows, group, lanes = ref.shape
    return ref.reshape(rows * group, lanes)[pl.ds(index, rows, stride=group), :]


def set_middle(ref, index, value):
    rows, group, lanes = ref.shape
    ref.reshape(rows * group, lanes)[pl.ds(index, rows, stride=group), :] = value


def project(p0, p1, p2):
    s = p1 * p1 + p2 * p2
    half = 0.5 * s
    lam = jnp.zeros_like(p0)
    for _ in range(NEWTON):
        growth = 1.0 + lam
        cube = growth * growth * growth
        lam = jnp.maximum(lam + ((p0 - lam) * cube + half * growth) / (cube + s), 0.0)
    inverse = 1.0 / (1.0 + lam)
    return p0 - lam, p1 * inverse, p2 * inverse


def kernel(
    sizes,
    mom_in, pot_in, rho_start, rho_end, ct, ctt, cy, cyt, et, et8, ey8,
    mom_out, pot_out,
    pot, hxp, hyp, hwt, hwx, hwy, face_x, face_y, wide, wt_last, wy_all,
    src, r1, s2, r2, sp, s3, r3, s4,
    ci, cg, rip, rra, fwd_out, fwd_in, back_out, back_in,
    halo_send, halo_recv, t_send, t_recv, y_send, y_recv, p_send, p_recv,
    local_sem,
):
    A, G, B, T, X, Y = sizes
    piece = X // A
    KT = NT // B
    pieces = G * A
    chunks = piece // ROWS
    blocks = T * X // 128
    planes = 128 // X
    ta, gx, gy = (lax.axis_index(name) for name in ("ta", "gx", "gy"))
    me = gx * A + ta

    def column(k):
        other = lax.rem(me + k, pieces)
        return other, (lax.rem(other, A), other // A, gy)

    def along_t(k):
        other = lax.rem(ta + k, A)
        return other, (other, gx, gy)

    def along_y(k):
        other = lax.rem(gy + k, B)
        return other, (ta, gx, other)

    def along_x(k):
        other = lax.rem(gx + k, G)
        return other, (ta, other, gy)

    barrier = pltpu.get_barrier_semaphore()

    @pl.loop(1, pieces)
    def _(k):
        pl.semaphore_signal(barrier, inc=1, device_id=column(k)[1], device_id_type=MESH)

    @pl.loop(1, B)
    def _(k):
        pl.semaphore_signal(barrier, inc=1, device_id=along_y(k)[1], device_id_type=MESH)

    pl.semaphore_wait(barrier, pieces + B - 2)

    row_x = lax.broadcasted_iota(jnp.int32, (X, Y), 0)
    lane_x = lax.broadcasted_iota(jnp.int32, (X, Y), 1)
    eye = lax.broadcasted_iota(jnp.int32, (128, 128), 0) == lax.broadcasted_iota(
        jnp.int32, (128, 128), 1
    )

    def pack_lane(read, lane):
        def step(n, _):
            value = jnp.broadcast_to(read(n)[:, lane : lane + 1], (128, 128))
            face_y[pl.ds(n, 1), :] = jnp.sum(
                jnp.where(eye, value, 0.0), axis=0, keepdims=True
            )
            return 0

        lax.fori_loop(0, blocks, step, 0)

    def unpack_lane(read):
        def step(n, _):
            value = jnp.broadcast_to(read(n), (128, 128))
            col = jnp.sum(jnp.where(eye, value, 0.0), axis=1, keepdims=True)
            wide[pl.ds(n * planes, planes), :, :] = jnp.broadcast_to(
                col, (128, 128)
            ).reshape(planes, X, Y)
            return 0

        lax.fori_loop(0, blocks, step, 0)

    @pl.loop(0, T)
    def _(t):
        pot[0, t] = pot_in[t]

    def coefficients(j, _):
        sigma = et[pl.ds(gy * KT, KT), :] + ey8[j][0:1, :]
        lanes = pl.ds(pl.multiple_of(j * 128, 128), 128)
        g = jnp.where(me == 0, 0.0, jnp.ones_like(sigma))
        h = sigma
        for i in range(piece - 1):
            inv = 1.0 / (g + 1.0 + h)
            g = g * inv
            ci[i, :, lanes] = inv
            cg[i, :, lanes] = g
            h = sigma + h * inv
        return 0

    lax.fori_loop(0, NY // 128, coefficients, 0)

    sigma = et8[gy * (KT // 4) + me // B] + ey8[lax.rem(me, B)]
    one = jnp.ones_like(sigma)

    def inner(i, state):
        g, h, h_first, ground = state
        inv = 1.0 / (g + 1.0 + h)
        inv_first = 1.0 / (1.0 + h_first)
        return (g * inv, sigma + h * inv, sigma + h_first * inv_first, ground + g * h * inv)

    link, h_end, h_first, ground = lax.fori_loop(
        0, piece - 1, inner, (one, sigma, sigma, jnp.zeros_like(sigma))
    )

    def outer(j, s):
        inv = 1.0 / (s + link)
        rip[j] = inv
        rra[j] = link * inv
        return jnp.where(j == pieces - 2, h_end, h_end + ground) + link * s * inv

    s_last = lax.fori_loop(0, pieces - 1, outer, h_first + ground)
    rip[pieces - 1] = jnp.where(
        s_last > 0.0, 1.0 / jnp.where(s_last > 0.0, s_last, 1.0), 0.0
    )

    def sweep(it, _):
        face_x[0] = middle(pot.at[it, pl.ds(0, T)], 0)
        pack_lane(
            lambda n: pot[it, pl.ds(n * planes, planes), :, :].reshape(128, 128), 0
        )

        def faces(phase, sources, targets, step):
            copies = []
            for n, (source, target, axis) in enumerate(
                zip(sources, targets, (along_t, along_x, along_y))
            ):
                copies.append(
                    pltpu.make_async_remote_copy(
                        src_ref=source,
                        dst_ref=target,
                        send_sem=halo_send.at[it, phase, n],
                        recv_sem=halo_recv.at[it, phase, n],
                        device_id=axis(step(axis))[1],
                        device_id_type=MESH,
                    )
                )
            for copy in copies:
                copy.start()
            return copies

        size_of = {along_t: A, along_x: G, along_y: B}
        copies = faces(
            0,
            (pot.at[it, 0], face_x.at[0], face_y),
            (pot.at[it, T], hxp.at[it], hyp.at[it]),
            lambda axis: size_of[axis] - 1,
        )
        for copy in copies:
            copy.wait()
        unpack_lane(lambda n: hyp[it, pl.ds(n, 1), :])

        def plane(t, before):
            here = pot[it, t]
            last_t = (ta == A - 1) & (t == T - 1)
            slope_t = jnp.where(last_t, 0.0, pot[it, t + 1] - here)
            nxt = jnp.where(
                row_x == X - 1, hxp[it, pl.ds(t, 1), :], pltpu.roll(here, X - 1, 0)
            )
            edge_x = (row_x == X - 1) & (gx == G - 1)
            slope_x = jnp.where(edge_x, 0.0, nxt - here)
            nxt = jnp.where(lane_x == Y - 1, wide[t], pltpu.roll(here, Y - 1, 1))
            edge_y = (lane_x == Y - 1) & (gy == B - 1)
            slope_y = jnp.where(edge_y, 0.0, nxt - here)
            m0, m1, m2 = (mom_out[a, t] for a in range(3))
            q0, q1, q2 = project(slope_t + m0, slope_x + m1, slope_y + m2)
            m0, m1, m2 = (m0 + (slope_t - q0), m1 + (slope_x - q1), m2 + (slope_y - q2))
            mom_out[0, t], mom_out[1, t], mom_out[2, t] = m0, m1, m2
            wt = jnp.where(last_t, 0.0, m0 - q0)
            wx = jnp.where(edge_x, 0.0, m1 - q1)
            wy = jnp.where(edge_y, 0.0, m2 - q2)
            wy_all[t] = wy
            face_x[1, pl.ds(t, 1), :] = wx[X - 1 : X, :]
            bound = jnp.where(last_t, rho_end[...], 0.0) - jnp.where(
                (ta == 0) & (t == 0), rho_start[...], 0.0
            )
            wx_back = jnp.where(row_x == 0, 0.0, pltpu.roll(wx, 1, 0))
            wy_back = jnp.where(lane_x == 0, 0.0, pltpu.roll(wy, 1, 1))
            src[t] = wt - before + (wx - wx_back) + (wy - wy_back) + bound
            return wt

        wt_last[...] = lax.fori_loop(0, T, plane, jnp.zeros((X, Y), jnp.float32))
        pack_lane(
            lambda n: wy_all[pl.ds(n * planes, planes), :, :].reshape(128, 128), Y - 1
        )

        copies = faces(
            1,
            (wt_last, face_x.at[1], face_y),
            (hwt.at[it], hwx.at[it], hwy.at[it]),
            lambda axis: 1,
        )
        for copy in copies:
            copy.wait()
        unpack_lane(lambda n: hwy[it, pl.ds(n, 1), :])

        def fix(t, _):
            value = src[t]
            value = value - jnp.where((t == 0) & (ta > 0), hwt[it], 0.0)
            value = value - jnp.where(
                (row_x == 0) & (gx > 0), hwx[it, pl.ds(t, 1), :], 0.0
            )
            src[t] = value - jnp.where((lane_x == 0) & (gy > 0), wide[t], 0.0)
            return 0

        lax.fori_loop(0, T, fix, 0)

        def exchange(phase, axis, count, c, source, target, sends, recvs):
            own = pltpu.make_async_copy(
                source(axis(0)[0], c), target(c), local_sem.at[it, phase, c]
            )
            own.start()
            copies = []
            for k in range(1, count):
                other, where = axis(k)
                copy = pltpu.make_async_remote_copy(
                    src_ref=source(other, c),
                    dst_ref=target(c),
                    send_sem=sends.at[it, phase // 2, c, k - 1],
                    recv_sem=recvs.at[it, phase // 2, c, k - 1],
                    device_id=where,
                    device_id_type=MESH,
                )
                copy.start()
                copies.append(copy)
            return own, copies

        def landed(pair):
            own, copies = pair
            own.wait()
            for copy in copies:
                copy.wait_recv()

        def sent(pairs):
            for _, copies in pairs:
                for copy in copies:
                    copy.wait_send()

        t_out = [
            exchange(
                0, along_t, A, c,
                lambda other, c: src.at[:, pl.ds(other * piece + c * ROWS, ROWS), :],
                lambda c: r1.at[it, pl.ds(ta * T, T), pl.ds(c * ROWS, ROWS), :],
                t_send, t_recv,
            )
            for c in range(chunks)
        ]
        y_out = []
        for c in range(chunks):
            landed(t_out[c])
            for x in range(c * ROWS, (c + 1) * ROWS, 2):
                pair = jnp.concatenate(
                    [middle(r1.at[it], x + d) for d in range(2)], axis=1
                )
                pair = matmul(ct[...], pair)
                s2[x] = pair[:, :Y]
                s2[x + 1] = pair[:, Y:]
            y_out.append(
                exchange(
                    1, along_y, B, c,
                    lambda other, c: s2.at[pl.ds(c * ROWS, ROWS), pl.ds(other * KT, KT), :],
                    lambda c: r2.at[
                        it, pl.ds(c * ROWS, ROWS), :, pl.ds(pl.multiple_of(gy * Y, Y), Y)
                    ],
                    y_send, y_recv,
                )
            )
        for c in range(chunks):
            landed(y_out[c])
            lines = pl.ds(c * ROWS, ROWS)
            sp[lines] = matmul(r2[it, lines].reshape(ROWS * KT, NY), cyt[...]).reshape(
                ROWS, KT, NY
            )

        def forward(j, _):
            lanes = pl.ds(pl.multiple_of(j * 128, 128), 128)
            value = sp[0, :, lanes]
            left = jnp.zeros_like(value)
            for i in range(piece - 1):
                left = left + cg[i, :, lanes] * value
                value = sp[i + 1, :, lanes] + ci[i, :, lanes] * value
                sp[i + 1, :, lanes] = value
            for q in range(KT // 4):
                part = slice(8 * (q // 2), 8 * (q // 2) + 8)
                a, b = left[part], value[part]
                low = lax.broadcasted_iota(jnp.int32, (8, 128), 0) < 4
                if q % 2:
                    tile = jnp.where(low, pltpu.roll(a, 4, 0), b)
                else:
                    tile = jnp.where(low, a, pltpu.roll(b, 4, 0))
                fwd_out[q * B + j, 0:8, :] = tile
            return 0

        inner_sum = jnp.zeros((8, 128), jnp.float32)
        for i in range(piece - 1):
            first = 0.5 * (piece * (piece - 1) - i * (i + 1))
            other = 0.5 * (i + 1) * (piece - 1 - i)
            inner_sum = inner_sum + jnp.where(me == 0, first, other) * sp[i, 0:8, 0:128]

        @pl.loop(0, pieces)
        def _(d):
            fwd_out[d, 8:16, :] = inner_sum

        lax.fori_loop(0, NY // 128, forward, 0)

        def scatter(phase, outgoing, incoming):
            def copy_of(k):
                other, where = column(k)
                return pltpu.make_async_remote_copy(
                    src_ref=outgoing.at[other],
                    dst_ref=incoming.at[it, me],
                    send_sem=p_send.at[it, phase, k - 1],
                    recv_sem=p_recv.at[it, phase, k - 1],
                    device_id=where,
                    device_id_type=MESH,
                )

            @pl.loop(1, pieces)
            def _(k):
                copy_of(k).start()

            incoming[it, me] = outgoing[me]

            @pl.loop(1, pieces)
            def _(k):
                copy_of(k).wait()

        scatter(0, fwd_out, fwd_in)

        def down(j, state):
            value, total = state
            back_out[j, 0:8, :] = value
            total = total + fwd_in[it, j + 1, 8:16, :]
            value = (
                fwd_in[it, j + 1, 0:8, :]
                + pltpu.roll(fwd_in[it, lax.rem(j + 2, pieces), 0:8, :], 4, 0)
                * jnp.where(j + 2 < pieces, 1.0, 0.0)
                + rra[j] * value
            )
            return value, total

        start = fwd_in[it, 0, 0:8, :] + pltpu.roll(fwd_in[it, 1, 0:8, :], 4, 0)
        value, total = lax.fori_loop(
            0, pieces - 1, down, (start, fwd_in[it, 0, 8:16, :])
        )
        full = value
        value = rip[pieces - 1] * value
        low = lax.broadcasted_iota(jnp.int32, (8, 128), 0) < 4
        weighted = value * (0.5 * (piece + 1))

        def up(n, state):
            value, weighted = state
            j = pieces - 2 - n
            before = rip[j] * back_out[j, 0:8, :] + rra[j] * value
            back_out[j + 1, 0:8, :] = jnp.where(low, pltpu.roll(before, 4, 0), value)
            weighted = weighted + before * jnp.where(
                j == 0, piece + 0.5 * (piece - 1), 1.0 * piece
            )
            return before, weighted

        value, weighted = lax.fori_loop(0, pieces - 1, up, (value, weighted))
        back_out[0, 0:8, :] = jnp.where(low, 0.0, value)
        excess = pltpu.roll(full, 4, 0)
        level = -(total + pltpu.roll(weighted, 4, 0)) / NX - excess * (
            (NX * NX - 1.0) / (6.0 * NX)
        )

        @pl.loop(0, pieces)
        def _(d):
            back_out[d, 8:16, :] = excess
            back_out[d, 16:24, :] = level

        scatter(1, back_out, back_in)

        def backward(j, _):
            lanes = pl.ds(pl.multiple_of(j * 128, 128), 128)
            left, value = [], []
            for half in range(KT // 8):
                a = back_in[it, 2 * half * B + j, 0:8, :]
                b = back_in[it, (2 * half + 1) * B + j, 0:8, :]
                left.append(jnp.where(low, a, pltpu.roll(b, 4, 0)))
                value.append(jnp.where(low, pltpu.roll(a, 4, 0), b))
            left = jnp.concatenate(left, axis=0)
            value = jnp.concatenate(value, axis=0)
            sp[piece - 1, :, lanes] = value
            for i in range(piece - 2, -1, -1):
                value = ci[i, :, lanes] * (sp[i, :, lanes] + value) + cg[i, :, lanes] * left
                sp[i, :, lanes] = value
            return 0

        lax.fori_loop(0, NY // 128, backward, 0)
        constant = (
            (gy == 0)
            & (lax.broadcasted_iota(jnp.int32, (8, 128), 0) == 0)
            & (lax.broadcasted_iota(jnp.int32, (8, 128), 1) == 0)
        )
        excess = back_in[it, 0, 8:16, :]
        level = back_in[it, 0, 16:24, :]
        for i in range(piece):
            cell = (me * piece + i).astype(jnp.float32)
            ramp = cell * (cell + 1.0) * (0.5 / NX)
            sp[i, 0:8, 0:128] += jnp.where(constant, excess * ramp + level, 0.0)

        y_back = []
        for c in range(chunks):
            lines = pl.ds(c * ROWS, ROWS)
            s3[lines] = matmul(sp[lines].reshape(ROWS * KT, NY), cy[...]).reshape(
                ROWS, KT, NY
            )
            y_back.append(
                exchange(
                    3, along_y, B, c,
                    lambda other, c: s3.at[
                        pl.ds(c * ROWS, ROWS), :, pl.ds(pl.multiple_of(other * Y, Y), Y)
                    ],
                    lambda c: r3.at[it, pl.ds(c * ROWS, ROWS), pl.ds(gy * KT, KT), :],
                    y_send, y_recv,
                )
            )
        t_back = []
        for c in range(chunks):
            landed(y_back[c])
            for x in range(c * ROWS, (c + 1) * ROWS, 2):
                pair = jnp.concatenate([r3[it, x + d] for d in range(2)], axis=1)
                pair = matmul(ctt[...], pair)
                set_middle(s4, x, pair[:, :Y])
                set_middle(s4, x + 1, pair[:, Y:])
            t_back.append(
                exchange(
                    2, along_t, A, c,
                    lambda other, c: s4.at[pl.ds(other * T, T), pl.ds(c * ROWS, ROWS), :],
                    lambda c: pot.at[
                        it + 1, pl.ds(0, T), pl.ds(ta * piece + c * ROWS, ROWS), :
                    ],
                    t_send, t_recv,
                )
            )
        for pair in t_back:
            landed(pair)
        for pairs in (t_out, y_out, y_back, t_back):
            sent(pairs)
        return 0

    @pl.loop(0, T)
    def _(t):
        for a in range(3):
            mom_out[a, t] = mom_in[a, t]

    lax.fori_loop(0, ITERS, sweep, 0)

    @pl.loop(0, T)
    def _(t):
        pot_out[t] = pot[ITERS, t]


def on_device(sizes, momenta, potential, rho_start, rho_end):
    A, G, B, T, X, Y = sizes
    piece, KT, pieces = X // A, NT // B, G * A
    assert Y == 128 and 128 % X == 0 and T * X % 128 == 0 and piece % ROWS == 0
    assert KT % 8 == 0 and pieces == (KT // 4) * B
    chunks = piece // ROWS
    table_t = cosine_table(NT).astype(np.float32)
    table_y = cosine_table(NY).astype(np.float32)
    e_t = eigenvalue(NT)
    spread_t = np.broadcast_to(e_t[:, None], (NT, 128)).astype(np.float32)
    spread_8 = np.broadcast_to(
        np.concatenate([e_t.reshape(NT // 4, 4)] * 2, axis=1)[:, :, None], (NT // 4, 8, 128)
    ).astype(np.float32)
    spread_y = np.broadcast_to(
        eigenvalue(NY).reshape(B, 1, 128), (B, 8, 128)
    ).astype(np.float32)
    tables = [table_t, table_t.T, table_y, table_y.T, spread_t, spread_8, spread_y]
    operands = [momenta, potential, rho_start, rho_end] + [
        jnp.asarray(np.ascontiguousarray(table)) for table in tables
    ]
    f32 = jnp.float32
    face = max(T * X // 128, 8)
    vmem = pl.BlockSpec(memory_space=pltpu.VMEM)
    dma = pltpu.SemaphoreType.DMA
    return pl.pallas_call(
        functools.partial(kernel, sizes),
        out_shape=(
            jax.ShapeDtypeStruct(momenta.shape, f32),
            jax.ShapeDtypeStruct(potential.shape, f32),
        ),
        in_specs=[vmem] * len(operands),
        out_specs=(vmem, vmem),
        scratch_shapes=[
            pltpu.VMEM((ITERS + 1, T + 1, X, Y), f32),
            pltpu.VMEM((ITERS, T, Y), f32),
            pltpu.VMEM((ITERS, face, 128), f32),
            pltpu.VMEM((ITERS, X, Y), f32),
            pltpu.VMEM((ITERS, T, Y), f32),
            pltpu.VMEM((ITERS, face, 128), f32),
            pltpu.VMEM((2, T, Y), f32),
            pltpu.VMEM((face, 128), f32),
            pltpu.VMEM((T, X, Y), f32),
            pltpu.VMEM((X, Y), f32),
            pltpu.VMEM((T, X, Y), f32),
            pltpu.VMEM((T, X, Y), f32),
            pltpu.VMEM((ITERS, NT, piece, Y), f32),
            pltpu.VMEM((piece, NT, Y), f32),
            pltpu.VMEM((ITERS, piece, KT, NY), f32),
            pltpu.VMEM((piece, KT, NY), f32),
            pltpu.VMEM((piece, KT, NY), f32),
            pltpu.VMEM((ITERS, piece, NT, Y), f32),
            pltpu.VMEM((NT, piece, Y), f32),
            pltpu.VMEM((piece, KT, NY), f32),
            pltpu.VMEM((piece, KT, NY), f32),
            pltpu.VMEM((pieces, 8, 128), f32),
            pltpu.VMEM((pieces, 8, 128), f32),
            pltpu.VMEM((pieces, 16, 128), f32),
            pltpu.VMEM((ITERS, pieces, 16, 128), f32),
            pltpu.VMEM((pieces, 24, 128), f32),
            pltpu.VMEM((ITERS, pieces, 24, 128), f32),
            dma((ITERS, 2, 3)),
            dma((ITERS, 2, 3)),
            dma((ITERS, 2, chunks, A - 1)),
            dma((ITERS, 2, chunks, A - 1)),
            dma((ITERS, 2, chunks, B - 1)),
            dma((ITERS, 2, chunks, B - 1)),
            dma((ITERS, 2, pieces - 1)),
            dma((ITERS, 2, pieces - 1)),
            dma((ITERS, 4, chunks)),
        ],
        compiler_params=pltpu.CompilerParams(
            collective_id=0, has_side_effects=True, vmem_limit_bytes=56 << 20
        ),
    )(*operands)


def solution(mesh):
    A, G, B = (mesh.shape[name] for name in ("ta", "gx", "gy"))
    sizes = (A, G, B, NT // A, NX // G, NY // B)
    placed = (P(None, "ta", "gx", "gy"), P("ta", "gx", "gy"), P("gx", "gy"), P("gx", "gy"))
    return jax.shard_map(
        functools.partial(on_device, sizes),
        mesh=mesh,
        in_specs=placed,
        out_specs=(P(None, "ta", "gx", "gy"), P("ta", "gx", "gy")),
        check_vma=False,
    )
```

```python
import functools

import jax
import jax.numpy as jnp
import numpy as np
from jax import lax
from jax.experimental import pallas as pl
from jax.experimental.pallas import tpu as pltpu
from jax.sharding import PartitionSpec as P

NT = 128
NX = 512
NY = 1024
ITERS = 2
NEWTON = 8
ROWS = 8

MESH = pl.DeviceIdType.MESH


def cosine_table(count):
    modes = np.arange(count, dtype=np.int64)[:, None]
    cells = np.arange(count, dtype=np.int64)[None, :]
    phase = modes * (2 * cells + 1) % (4 * count)
    weight = np.where(modes == 0, 1.0, 2.0) / count
    return np.sqrt(weight) * np.cos(phase * (np.pi / (2 * count)))


def eigenvalue(count):
    return (2.0 * np.sin(np.arange(count) * (np.pi / (2 * count)))) ** 2


def matmul(left, right):
    return jnp.dot(
        left, right, precision=lax.Precision.HIGHEST, preferred_element_type=jnp.float32
    )


def middle(ref, index):
    rows, group, lanes = ref.shape
    return ref.reshape(rows * group, lanes)[pl.ds(index, rows, stride=group), :]


def set_middle(ref, index, value):
    rows, group, lanes = ref.shape
    ref.reshape(rows * group, lanes)[pl.ds(index, rows, stride=group), :] = value


def project(p0, p1, p2):
    s = p1 * p1 + p2 * p2
    half = 0.5 * s
    lam = jnp.zeros_like(p0)
    for _ in range(NEWTON):
        growth = 1.0 + lam
        cube = growth * growth * growth
        lam = jnp.maximum(lam + ((p0 - lam) * cube + half * growth) / (cube + s), 0.0)
    inverse = 1.0 / (1.0 + lam)
    return p0 - lam, p1 * inverse, p2 * inverse


def kernel(
    sizes,
    mom_in, pot_in, rho_start, rho_end, ct, ctt, cy, cyt, et, et8, ey8,
    mom_out, pot_out,
    pot, hxp, hyp, hwt, hwx, hwy, face_x, face_y, wide, wt_last, wy_all,
    src, r1, s2, r2, sp, s3, r3, s4,
    ci, cg, rip, rra, fwd_out, fwd_in, back_out, back_in, extra_out, extra_in,
    halo_send, halo_recv, t_send, t_recv, y_send, y_recv, p_send, p_recv, e_send, e_recv,
    local_sem,
):
    A, G, B, T, X, Y = sizes
    piece = X // A
    KT = NT // B
    pieces = G * A
    chunks = piece // ROWS
    blocks = T * X // 128
    planes = 128 // X
    unroll = min(blocks, 4)
    ta, gx, gy = (lax.axis_index(name) for name in ("ta", "gx", "gy"))
    me = gx * A + ta

    def column(k):
        other = lax.rem(me + k, pieces)
        return other, (lax.rem(other, A), other // A, gy)

    def along_t(k):
        other = lax.rem(ta + k, A)
        return other, (other, gx, gy)

    def along_y(k):
        other = lax.rem(gy + k, B)
        return other, (ta, gx, other)

    def along_x(k):
        other = lax.rem(gx + k, G)
        return other, (ta, other, gy)

    barrier = pltpu.get_barrier_semaphore()

    @pl.loop(1, pieces)
    def _(k):
        pl.semaphore_signal(barrier, inc=1, device_id=column(k)[1], device_id_type=MESH)

    @pl.loop(1, B)
    def _(k):
        pl.semaphore_signal(barrier, inc=1, device_id=along_y(k)[1], device_id_type=MESH)

    pl.semaphore_wait(barrier, pieces + B - 2)

    row_x = lax.broadcasted_iota(jnp.int32, (X, Y), 0)
    lane_x = lax.broadcasted_iota(jnp.int32, (X, Y), 1)
    eye = lax.broadcasted_iota(jnp.int32, (128, 128), 0) == lax.broadcasted_iota(
        jnp.int32, (128, 128), 1
    )

    def pack_lane(read, lane):
        def step(group, _):
            for u in range(unroll):
                n = group * unroll + u
                value = jnp.broadcast_to(read(n)[:, lane : lane + 1], (128, 128))
                face_y[pl.ds(n, 1), :] = jnp.sum(
                    jnp.where(eye, value, 0.0), axis=0, keepdims=True
                )
            return 0

        lax.fori_loop(0, blocks // unroll, step, 0)

    def unpack_lane(read):
        def step(group, _):
            for u in range(unroll):
                n = group * unroll + u
                value = jnp.broadcast_to(read(n), (128, 128))
                col = jnp.sum(jnp.where(eye, value, 0.0), axis=1, keepdims=True)
                wide[pl.ds(n * planes, planes), :, :] = jnp.broadcast_to(
                    col, (128, 128)
                ).reshape(planes, X, Y)
            return 0

        lax.fori_loop(0, blocks // unroll, step, 0)

    @pl.loop(0, T)
    def _(t):
        pot[0, t] = pot_in[t]

    def prepare():
        def coefficients(j, _):
            sigma = et[pl.ds(gy * KT, KT), :] + ey8[j][0:1, :]
            lanes = pl.ds(pl.multiple_of(j * 128, 128), 128)
            g = jnp.where(me == 0, 0.0, jnp.ones_like(sigma))
            h = sigma
            for i in range(piece - 1):
                inv = 1.0 / (g + 1.0 + h)
                g = g * inv
                ci[i, :, lanes] = inv
                cg[i, :, lanes] = g
                h = sigma + h * inv
            return 0

        lax.fori_loop(0, NY // 128, coefficients, 0)

        sigma = et8[gy * (KT // 4) + me // B] + ey8[lax.rem(me, B)]
        one = jnp.ones_like(sigma)

        def inner(i, state):
            g, h, h_first, ground = state
            inv = 1.0 / (g + 1.0 + h)
            inv_first = 1.0 / (1.0 + h_first)
            return (g * inv, sigma + h * inv, sigma + h_first * inv_first, ground + g * h * inv)

        link, h_end, h_first, ground = lax.fori_loop(
            0, piece - 1, inner, (one, sigma, sigma, jnp.zeros_like(sigma))
        )

        def outer(j, s):
            inv = 1.0 / (s + link)
            rip[j] = inv
            rra[j] = link * inv
            return jnp.where(j == pieces - 2, h_end, h_end + ground) + link * s * inv

        s_last = lax.fori_loop(0, pieces - 1, outer, h_first + ground)
        rip[pieces - 1] = jnp.where(
            s_last > 0.0, 1.0 / jnp.where(s_last > 0.0, s_last, 1.0), 0.0
        )

    def sweep(it, _):
        face_x[0] = middle(pot.at[it, pl.ds(0, T)], 0)
        pack_lane(
            lambda n: pot[it, pl.ds(n * planes, planes), :, :].reshape(128, 128), 0
        )

        def faces(phase, sources, targets, step):
            copies = []
            for n, (source, target, axis) in enumerate(
                zip(sources, targets, (along_t, along_x, along_y))
            ):
                copies.append(
                    pltpu.make_async_remote_copy(
                        src_ref=source,
                        dst_ref=target,
                        send_sem=halo_send.at[it, phase, n],
                        recv_sem=halo_recv.at[it, phase, n],
                        device_id=axis(step(axis))[1],
                        device_id_type=MESH,
                    )
                )
            for copy in copies:
                copy.start()
            return copies

        size_of = {along_t: A, along_x: G, along_y: B}
        copies = faces(
            0,
            (pot.at[it, 0], face_x.at[0], face_y),
            (pot.at[it, T], hxp.at[it], hyp.at[it]),
            lambda axis: size_of[axis] - 1,
        )
        pl.when(it == 0)(prepare)
        for copy in copies:
            copy.wait()
        unpack_lane(lambda n: hyp[it, pl.ds(n, 1), :])

        def plane(t, before):
            here = pot[it, t]
            last_t = (ta == A - 1) & (t == T - 1)
            slope_t = jnp.where(last_t, 0.0, pot[it, t + 1] - here)
            nxt = jnp.where(
                row_x == X - 1, hxp[it, pl.ds(t, 1), :], pltpu.roll(here, X - 1, 0)
            )
            edge_x = (row_x == X - 1) & (gx == G - 1)
            slope_x = jnp.where(edge_x, 0.0, nxt - here)
            nxt = jnp.where(lane_x == Y - 1, wide[t], pltpu.roll(here, Y - 1, 1))
            edge_y = (lane_x == Y - 1) & (gy == B - 1)
            slope_y = jnp.where(edge_y, 0.0, nxt - here)
            m0, m1, m2 = (mom_out[a, t] for a in range(3))
            q0, q1, q2 = project(slope_t + m0, slope_x + m1, slope_y + m2)
            m0, m1, m2 = (m0 + (slope_t - q0), m1 + (slope_x - q1), m2 + (slope_y - q2))
            mom_out[0, t], mom_out[1, t], mom_out[2, t] = m0, m1, m2
            wt = jnp.where(last_t, 0.0, m0 - q0)
            wx = jnp.where(edge_x, 0.0, m1 - q1)
            wy = jnp.where(edge_y, 0.0, m2 - q2)
            wy_all[t] = wy
            face_x[1, pl.ds(t, 1), :] = wx[X - 1 : X, :]
            bound = jnp.where(last_t, rho_end[...], 0.0) - jnp.where(
                (ta == 0) & (t == 0), rho_start[...], 0.0
            )
            wx_back = jnp.where(row_x == 0, 0.0, pltpu.roll(wx, 1, 0))
            wy_back = jnp.where(lane_x == 0, 0.0, pltpu.roll(wy, 1, 1))
            src[t] = wt - before + (wx - wx_back) + (wy - wy_back) + bound
            return wt

        wt_last[...] = lax.fori_loop(0, T, plane, jnp.zeros((X, Y), jnp.float32))
        pack_lane(
            lambda n: wy_all[pl.ds(n * planes, planes), :, :].reshape(128, 128), Y - 1
        )

        copies = faces(
            1,
            (wt_last, face_x.at[1], face_y),
            (hwt.at[it], hwx.at[it], hwy.at[it]),
            lambda axis: 1,
        )
        for copy in copies:
            copy.wait()
        unpack_lane(lambda n: hwy[it, pl.ds(n, 1), :])

        def fix(t, _):
            value = src[t]
            value = value - jnp.where((t == 0) & (ta > 0), hwt[it], 0.0)
            value = value - jnp.where(
                (row_x == 0) & (gx > 0), hwx[it, pl.ds(t, 1), :], 0.0
            )
            src[t] = value - jnp.where((lane_x == 0) & (gy > 0), wide[t], 0.0)
            return 0

        lax.fori_loop(0, T, fix, 0)

        def exchange(phase, axis, count, c, source, target, sends, recvs):
            own = pltpu.make_async_copy(
                source(axis(0)[0], c), target(c), local_sem.at[it, phase, c]
            )
            own.start()
            copies = []
            for k in range(1, count):
                other, where = axis(k)
                copy = pltpu.make_async_remote_copy(
                    src_ref=source(other, c),
                    dst_ref=target(c),
                    send_sem=sends.at[it, phase // 2, c, k - 1],
                    recv_sem=recvs.at[it, phase // 2, c, k - 1],
                    device_id=where,
                    device_id_type=MESH,
                )
                copy.start()
                copies.append(copy)
            return own, copies

        def landed(pair):
            own, copies = pair
            own.wait()
            for copy in copies:
                copy.wait_recv()

        def sent(pairs):
            for _, copies in pairs:
                for copy in copies:
                    copy.wait_send()

        t_out = [
            exchange(
                0, along_t, A, c,
                lambda other, c: src.at[:, pl.ds(other * piece + c * ROWS, ROWS), :],
                lambda c: r1.at[it, pl.ds(ta * T, T), pl.ds(c * ROWS, ROWS), :],
                t_send, t_recv,
            )
            for c in range(chunks)
        ]
        y_out = []
        for c in range(chunks):
            landed(t_out[c])
            for x in range(c * ROWS, (c + 1) * ROWS, 2):
                pair = jnp.concatenate(
                    [middle(r1.at[it], x + d) for d in range(2)], axis=1
                )
                pair = matmul(ct[...], pair)
                s2[x] = pair[:, :Y]
                s2[x + 1] = pair[:, Y:]
            y_out.append(
                exchange(
                    1, along_y, B, c,
                    lambda other, c: s2.at[pl.ds(c * ROWS, ROWS), pl.ds(other * KT, KT), :],
                    lambda c: r2.at[
                        it, pl.ds(c * ROWS, ROWS), :, pl.ds(pl.multiple_of(gy * Y, Y), Y)
                    ],
                    y_send, y_recv,
                )
            )
        for c in range(chunks):
            landed(y_out[c])
            lines = pl.ds(c * ROWS, ROWS)
            sp[lines] = matmul(r2[it, lines].reshape(ROWS * KT, NY), cyt[...]).reshape(
                ROWS, KT, NY
            )

        def forward(j, _):
            lanes = pl.ds(pl.multiple_of(j * 128, 128), 128)
            value = sp[0, :, lanes]
            left = jnp.zeros_like(value)
            for i in range(piece - 1):
                left = left + cg[i, :, lanes] * value
                value = sp[i + 1, :, lanes] + ci[i, :, lanes] * value
                sp[i + 1, :, lanes] = value
            for q in range(KT // 4):
                part = slice(8 * (q // 2), 8 * (q // 2) + 8)
                a, b = left[part], value[part]
                low = lax.broadcasted_iota(jnp.int32, (8, 128), 0) < 4
                if q % 2:
                    tile = jnp.where(low, pltpu.roll(a, 4, 0), b)
                else:
                    tile = jnp.where(low, a, pltpu.roll(b, 4, 0))
                fwd_out[q * B + j] = tile
            return 0

        inner_sum = jnp.zeros((8, 128), jnp.float32)
        for i in range(piece - 1):
            first = 0.5 * (piece * (piece - 1) - i * (i + 1))
            other = 0.5 * (i + 1) * (piece - 1 - i)
            inner_sum = inner_sum + jnp.where(me == 0, first, other) * sp[i, 0:8, 0:128]

        extra_out[0] = inner_sum
        lax.fori_loop(0, NY // 128, forward, 0)

        partners = [(dx, dt) for dx in range(G) for dt in range(A)][1:]
        to_x = [lax.rem(gx + d, G) for d in range(G)]
        to_t = [lax.rem(ta + d, A) for d in range(A)]

        def scatter(phase, outgoing, incoming):
            copies = []
            for n, (dx, dt) in enumerate(partners):
                copies.append(
                    pltpu.make_async_remote_copy(
                        src_ref=outgoing.at[to_x[dx] * A + to_t[dt]],
                        dst_ref=incoming.at[it, me],
                        send_sem=p_send.at[it, phase, n],
                        recv_sem=p_recv.at[it, phase, n],
                        device_id=(to_t[dt], to_x[dx], gy),
                        device_id_type=MESH,
                    )
                )
            for copy in copies:
                copy.start()
            incoming[it, me] = outgoing[me]
            return copies

        def gather_copy(k):
            return pltpu.make_async_remote_copy(
                src_ref=extra_out.at[0],
                dst_ref=extra_in.at[it, k],
                send_sem=e_send.at[it, k],
                recv_sem=e_recv.at[it, k],
                device_id=(0, 0, gy),
                device_id_type=MESH,
            )

        def spread_copy(k):
            return pltpu.make_async_remote_copy(
                src_ref=extra_out.at[1],
                dst_ref=extra_in.at[it, pieces],
                send_sem=e_send.at[it, k],
                recv_sem=e_recv.at[it, pieces],
                device_id=(lax.rem(k, A), k // A, gy),
                device_id_type=MESH,
            )

        head = (gy == 0) & (me == 0)
        tail = (gy == 0) & (me > 0)
        copies = scatter(0, fwd_out, fwd_in)

        @pl.when(tail)
        def _():
            gather_copy(me).start()

        @pl.when(head)
        def _():
            extra_in[it, 0] = extra_out[0]

            @pl.loop(1, pieces)
            def _(k):
                gather_copy(k).wait_recv()

        for copy in copies:
            copy.wait_recv()

        low = lax.broadcasted_iota(jnp.int32, (8, 128), 0) < 4
        value = fwd_in[it, 0] + pltpu.roll(fwd_in[it, 1], 4, 0)
        before = [value]
        for j in range(1, pieces):
            given = fwd_in[it, j]
            if j + 1 < pieces:
                given = given + pltpu.roll(fwd_in[it, j + 1], 4, 0)
            value = given + rra[j - 1] * value
            before.append(value)
        full = value
        value = rip[pieces - 1] * value
        weighted = value * (0.5 * (piece + 1))
        for j in range(pieces - 2, -1, -1):
            here = rip[j] * before[j] + rra[j] * value
            back_out[j + 1] = jnp.where(low, pltpu.roll(here, 4, 0), value)
            value = here
            weighted = weighted + value * (
                piece + 0.5 * (piece - 1) if j == 0 else 1.0 * piece
            )
        back_out[0] = jnp.where(low, 0.0, value)
        returns = scatter(1, back_out, back_in)

        @pl.when(head)
        def _():
            total = lax.fori_loop(
                1, pieces, lambda k, acc: acc + extra_in[it, k], extra_in[it, 0]
            )
            excess = pltpu.roll(full, 4, 0)
            level = -(total + pltpu.roll(weighted, 4, 0)) / NX - excess * (
                (NX * NX - 1.0) / (6.0 * NX)
            )
            row = lax.broadcasted_iota(jnp.int32, (8, 128), 0)
            extra_out[1] = jnp.where(row == 0, excess, pltpu.roll(level, 1, 0))
            extra_in[it, pieces] = extra_out[1]

            @pl.loop(1, pieces)
            def _(k):
                spread_copy(k).start()

        for copy in returns:
            copy.wait_recv()

        @pl.when(tail)
        def _():
            spread_copy(me).wait_recv()

        def backward(j, _):
            lanes = pl.ds(pl.multiple_of(j * 128, 128), 128)
            left, value = [], []
            for half in range(KT // 8):
                a = back_in[it, 2 * half * B + j]
                b = back_in[it, (2 * half + 1) * B + j]
                left.append(jnp.where(low, a, pltpu.roll(b, 4, 0)))
                value.append(jnp.where(low, pltpu.roll(a, 4, 0), b))
            left = jnp.concatenate(left, axis=0)
            value = jnp.concatenate(value, axis=0)
            sp[piece - 1, :, lanes] = value
            for i in range(piece - 2, -1, -1):
                value = ci[i, :, lanes] * (sp[i, :, lanes] + value) + cg[i, :, lanes] * left
                sp[i, :, lanes] = value
            return 0

        lax.fori_loop(0, NY // 128, backward, 0)

        @pl.when(gy == 0)
        def _():
            row = lax.broadcasted_iota(jnp.int32, (8, 128), 0)
            constant = (row == 0) & (lax.broadcasted_iota(jnp.int32, (8, 128), 1) == 0)
            excess = extra_in[it, pieces]
            level = pltpu.roll(excess, 7, 0)
            for i in range(piece):
                cell = (me * piece + i).astype(jnp.float32)
                ramp = cell * (cell + 1.0) * (0.5 / NX)
                sp[i, 0:8, 0:128] += jnp.where(constant, excess * ramp + level, 0.0)

        y_back = []
        for c in range(chunks):
            lines = pl.ds(c * ROWS, ROWS)
            s3[lines] = matmul(sp[lines].reshape(ROWS * KT, NY), cy[...]).reshape(
                ROWS, KT, NY
            )
            y_back.append(
                exchange(
                    3, along_y, B, c,
                    lambda other, c: s3.at[
                        pl.ds(c * ROWS, ROWS), :, pl.ds(pl.multiple_of(other * Y, Y), Y)
                    ],
                    lambda c: r3.at[it, pl.ds(c * ROWS, ROWS), pl.ds(gy * KT, KT), :],
                    y_send, y_recv,
                )
            )
        t_back = []
        for c in range(chunks):
            landed(y_back[c])
            for x in range(c * ROWS, (c + 1) * ROWS, 2):
                pair = jnp.concatenate([r3[it, x + d] for d in range(2)], axis=1)
                pair = matmul(ctt[...], pair)
                set_middle(s4, x, pair[:, :Y])
                set_middle(s4, x + 1, pair[:, Y:])
            t_back.append(
                exchange(
                    2, along_t, A, c,
                    lambda other, c: s4.at[pl.ds(other * T, T), pl.ds(c * ROWS, ROWS), :],
                    lambda c: pot.at[
                        it + 1, pl.ds(0, T), pl.ds(ta * piece + c * ROWS, ROWS), :
                    ],
                    t_send, t_recv,
                )
            )
        for pair in t_back:
            landed(pair)
        for pairs in (t_out, y_out, y_back, t_back):
            sent(pairs)
        for copy in copies + returns:
            copy.wait_send()

        @pl.when(tail)
        def _():
            gather_copy(me).wait_send()

        @pl.when(head)
        def _():
            @pl.loop(1, pieces)
            def _(k):
                spread_copy(k).wait_send()

        return 0

    @pl.loop(0, T)
    def _(t):
        for a in range(3):
            mom_out[a, t] = mom_in[a, t]

    lax.fori_loop(0, ITERS, sweep, 0)

    @pl.loop(0, T)
    def _(t):
        pot_out[t] = pot[ITERS, t]


def on_device(sizes, momenta, potential, rho_start, rho_end):
    A, G, B, T, X, Y = sizes
    piece, KT, pieces = X // A, NT // B, G * A
    assert Y == 128 and 128 % X == 0 and T * X % 128 == 0 and piece % ROWS == 0
    assert KT % 8 == 0 and pieces == (KT // 4) * B
    chunks = piece // ROWS
    table_t = cosine_table(NT).astype(np.float32)
    table_y = cosine_table(NY).astype(np.float32)
    e_t = eigenvalue(NT)
    spread_t = np.broadcast_to(e_t[:, None], (NT, 128)).astype(np.float32)
    spread_8 = np.broadcast_to(
        np.concatenate([e_t.reshape(NT // 4, 4)] * 2, axis=1)[:, :, None], (NT // 4, 8, 128)
    ).astype(np.float32)
    spread_y = np.broadcast_to(
        eigenvalue(NY).reshape(B, 1, 128), (B, 8, 128)
    ).astype(np.float32)
    tables = [table_t, table_t.T, table_y, table_y.T, spread_t, spread_8, spread_y]
    operands = [momenta, potential, rho_start, rho_end] + [
        jnp.asarray(np.ascontiguousarray(table)) for table in tables
    ]
    f32 = jnp.float32
    face = max(T * X // 128, 8)
    vmem = pl.BlockSpec(memory_space=pltpu.VMEM)
    dma = pltpu.SemaphoreType.DMA
    return pl.pallas_call(
        functools.partial(kernel, sizes),
        out_shape=(
            jax.ShapeDtypeStruct(momenta.shape, f32),
            jax.ShapeDtypeStruct(potential.shape, f32),
        ),
        in_specs=[vmem] * len(operands),
        out_specs=(vmem, vmem),
        scratch_shapes=[
            pltpu.VMEM((ITERS + 1, T + 1, X, Y), f32),
            pltpu.VMEM((ITERS, T, Y), f32),
            pltpu.VMEM((ITERS, face, 128), f32),
            pltpu.VMEM((ITERS, X, Y), f32),
            pltpu.VMEM((ITERS, T, Y), f32),
            pltpu.VMEM((ITERS, face, 128), f32),
            pltpu.VMEM((2, T, Y), f32),
            pltpu.VMEM((face, 128), f32),
            pltpu.VMEM((T, X, Y), f32),
            pltpu.VMEM((X, Y), f32),
            pltpu.VMEM((T, X, Y), f32),
            pltpu.VMEM((T, X, Y), f32),
            pltpu.VMEM((ITERS, NT, piece, Y), f32),
            pltpu.VMEM((piece, NT, Y), f32),
            pltpu.VMEM((ITERS, piece, KT, NY), f32),
            pltpu.VMEM((piece, KT, NY), f32),
            pltpu.VMEM((piece, KT, NY), f32),
            pltpu.VMEM((ITERS, piece, NT, Y), f32),
            pltpu.VMEM((NT, piece, Y), f32),
            pltpu.VMEM((piece, KT, NY), f32),
            pltpu.VMEM((piece, KT, NY), f32),
            pltpu.VMEM((pieces, 8, 128), f32),
            pltpu.VMEM((pieces, 8, 128), f32),
            pltpu.VMEM((pieces, 8, 128), f32),
            pltpu.VMEM((ITERS, pieces, 8, 128), f32),
            pltpu.VMEM((pieces, 8, 128), f32),
            pltpu.VMEM((ITERS, pieces, 8, 128), f32),
            pltpu.VMEM((2, 8, 128), f32),
            pltpu.VMEM((ITERS, pieces + 1, 8, 128), f32),
            dma((ITERS, 2, 3)),
            dma((ITERS, 2, 3)),
            dma((ITERS, 2, chunks, A - 1)),
            dma((ITERS, 2, chunks, A - 1)),
            dma((ITERS, 2, chunks, B - 1)),
            dma((ITERS, 2, chunks, B - 1)),
            dma((ITERS, 2, pieces - 1)),
            dma((ITERS, 2, pieces - 1)),
            dma((ITERS, pieces)),
            dma((ITERS, pieces + 1)),
            dma((ITERS, 4, chunks)),
        ],
        compiler_params=pltpu.CompilerParams(
            collective_id=0, has_side_effects=True, vmem_limit_bytes=56 << 20
        ),
    )(*operands)


def solution(mesh):
    A, G, B = (mesh.shape[name] for name in ("ta", "gx", "gy"))
    sizes = (A, G, B, NT // A, NX // G, NY // B)
    placed = (P(None, "ta", "gx", "gy"), P("ta", "gx", "gy"), P("gx", "gy"), P("gx", "gy"))
    return jax.shard_map(
        functools.partial(on_device, sizes),
        mesh=mesh,
        in_specs=placed,
        out_specs=(P(None, "ta", "gx", "gy"), P("ta", "gx", "gy")),
        check_vma=False,
    )
```

```python
import functools

import jax
import jax.numpy as jnp
import numpy as np
from jax import lax
from jax.experimental import pallas as pl
from jax.experimental.pallas import tpu as pltpu
from jax.sharding import PartitionSpec as P

NT = 128
NX = 512
NY = 1024
ITERS = 2
NEWTON = 8
ROWS = 4

MESH = pl.DeviceIdType.MESH


def cosine_table(count):
    modes = np.arange(count, dtype=np.int64)[:, None]
    cells = np.arange(count, dtype=np.int64)[None, :]
    phase = modes * (2 * cells + 1) % (4 * count)
    weight = np.where(modes == 0, 1.0, 2.0) / count
    return np.sqrt(weight) * np.cos(phase * (np.pi / (2 * count)))


def eigenvalue(count):
    return (2.0 * np.sin(np.arange(count) * (np.pi / (2 * count)))) ** 2


def split(value):
    parts = []
    for _ in range(3):
        part = value.astype(jnp.bfloat16)
        parts.append(part)
        value = value - part.astype(jnp.float32)
    return parts


def product(left, right):
    return jnp.dot(left, right, preferred_element_type=jnp.float32)


def table_right(value, table):
    rows = value.shape[0]
    parts = split(value)
    total = product(parts[0], table[2])
    middle_ = product(jnp.concatenate(parts[:2], axis=0), table[1])
    large = product(jnp.concatenate(parts, axis=0), table[0])
    total = total + (middle_[rows:] + large[2 * rows :])
    total = total + (middle_[:rows] + large[rows : 2 * rows])
    return total + large[:rows]


def table_left(table, value):
    rows = table.shape[0] // 3
    parts = split(value)
    total = product(table[:rows], parts[2])
    middle_ = product(table[: 2 * rows], parts[1])
    large = product(table[...], parts[0])
    total = total + (middle_[rows:] + large[2 * rows :])
    total = total + (middle_[:rows] + large[rows : 2 * rows])
    return total + large[:rows]


def middle(ref, index):
    rows, group, lanes = ref.shape
    return ref.reshape(rows * group, lanes)[pl.ds(index, rows, stride=group), :]


def set_middle(ref, index, value):
    rows, group, lanes = ref.shape
    ref.reshape(rows * group, lanes)[pl.ds(index, rows, stride=group), :] = value


def project(p0, p1, p2):
    s = p1 * p1 + p2 * p2
    half = 0.5 * s
    lam = jnp.zeros_like(p0)
    for _ in range(NEWTON):
        growth = 1.0 + lam
        cube = growth * growth * growth
        lam = jnp.maximum(lam + ((p0 - lam) * cube + half * growth) / (cube + s), 0.0)
    inverse = 1.0 / (1.0 + lam)
    return p0 - lam, p1 * inverse, p2 * inverse


def kernel(
    sizes,
    mom_hbm, pot_in, rho_start, rho_end, ct_hbm, ctt_hbm, cy_hbm, cyt_hbm, et, et8, ey8,
    mom_out, pot_out,
    momv, momx, ct, ctt, cy, cyt,
    pot, ht, hyp, hwt, hwx, hwy, face_p, face_t, face_y, ht_out, wx_all, src,
    r1, s2, r2, sp, sq, s3, r3, s4, ci, cg, rip, rra,
    fwd_out, fwd_in, back_out, back_in, extra_out, extra_in,
    load_sem, halo_send, halo_recv, w_send, w_recv, th_send, th_recv, xh_send, xh_recv,
    t_send, t_recv, y_send, y_recv, p_send, p_recv, e_send, e_recv, local_sem,
):
    A, G, B, T, X, Y = sizes
    piece = X // A
    KT = NT // B
    pieces = G * A
    stages = piece // ROWS
    groups = X // ROWS
    high = ROWS * T
    ta, gx, gy = (lax.axis_index(name) for name in ("ta", "gx", "gy"))
    me = gx * A + ta
    to_t = [lax.rem(ta + d, A) for d in range(A)]
    to_x = [lax.rem(gx + d, G) for d in range(G)]
    to_y = [lax.rem(gy + d, B) for d in range(B)]
    partners = [(dx, dt) for dx in range(G) for dt in range(A)][1:]

    def remote(source, target, send, recv, where):
        return pltpu.make_async_remote_copy(
            src_ref=source, dst_ref=target, send_sem=send, recv_sem=recv,
            device_id=where, device_id_type=MESH,
        )

    loads = [
        pltpu.make_async_copy(source, target, load_sem.at[n])
        for n, (source, target) in enumerate(
            ((mom_hbm, momv), (ct_hbm, ct), (cyt_hbm, cyt), (cy_hbm, cy), (ctt_hbm, ctt))
        )
    ]
    for load in loads:
        load.start()

    barrier = pltpu.get_barrier_semaphore()
    for dx, dt in partners:
        pl.semaphore_signal(
            barrier, inc=1, device_id=(to_t[dt], to_x[dx], gy), device_id_type=MESH
        )
    for d in range(1, B):
        pl.semaphore_signal(
            barrier, inc=1, device_id=(ta, gx, to_y[d]), device_id_type=MESH
        )

    sub = lax.broadcasted_iota(jnp.int32, (high, Y), 0)
    lane = lax.broadcasted_iota(jnp.int32, (high, Y), 1)
    eye = sub == lane
    time = lax.rem(sub, T)
    low = lax.broadcasted_iota(jnp.int32, (8, 128), 0) < 4

    def pack(column):
        spread = jnp.broadcast_to(column, (high, Y))
        return jnp.sum(jnp.where(eye, spread, 0.0), axis=0, keepdims=True)

    def unpack(row):
        spread = jnp.broadcast_to(row, (high, Y))
        return jnp.sum(jnp.where(eye, spread, 0.0), axis=1, keepdims=True)

    def rows_of(parts):
        return jnp.concatenate([jnp.broadcast_to(p, (T, Y)) for p in parts], axis=0)

    def pack_first(it, n):
        value = pot[it, pl.ds(n * ROWS, ROWS), :, :].reshape(high, Y)
        face_p[it, pl.ds(n, 1), :] = pack(value[:, 0:1])

    def first(n, _):
        for r in range(ROWS):
            pot[0, n * ROWS + r] = middle(pot_in, n * ROWS + r)
        pack_first(0, n)
        return 0

    lax.fori_loop(0, groups, first, 0)
    pl.semaphore_wait(barrier, pieces + B - 2)

    def prepare():
        def coefficients(j, _):
            sigma = et[pl.ds(gy * KT, KT), :] + ey8[j][0:1, :]
            lanes = pl.ds(pl.multiple_of(j * 128, 128), 128)
            g = jnp.where(me == 0, 0.0, jnp.ones_like(sigma))
            h = sigma
            for i in range(piece - 1):
                inv = 1.0 / (g + 1.0 + h)
                g = g * inv
                ci[i, :, lanes] = inv
                cg[i, :, lanes] = g
                h = sigma + h * inv
            return 0

        lax.fori_loop(0, NY // 128, coefficients, 0)

        sigma = et8[gy * (KT // 4) + me // B] + ey8[lax.rem(me, B)]
        one = jnp.ones_like(sigma)

        def inner(i, state):
            g, h, h_first, ground = state
            inv = 1.0 / (g + 1.0 + h)
            inv_first = 1.0 / (1.0 + h_first)
            return (
                g * inv, sigma + h * inv, sigma + h_first * inv_first, ground + g * h * inv
            )

        link, h_end, h_first, ground = lax.fori_loop(
            0, piece - 1, inner, (one, sigma, sigma, jnp.zeros_like(sigma))
        )

        def outer(j, s):
            inv = 1.0 / (s + link)
            rip[j] = inv
            rra[j] = link * inv
            return jnp.where(j == pieces - 2, h_end, h_end + ground) + link * s * inv

        s_last = lax.fori_loop(0, pieces - 1, outer, h_first + ground)
        rip[pieces - 1] = jnp.where(
            s_last > 0.0, 1.0 / jnp.where(s_last > 0.0, s_last, 1.0), 0.0
        )

    def exchange(it, way, c, own, others, sends, recvs):
        local = pltpu.make_async_copy(*own, local_sem.at[it, way, c])
        local.start()
        copies = [
            remote(source, target, sends.at[it, way // 2, c, k], recvs.at[it, way // 2, c, k], where)
            for k, (source, target, where) in enumerate(others)
        ]
        for copy in copies:
            copy.start()
        return local, copies

    def along_t(it, way, c, source, target):
        return exchange(
            it, way, c, (source(ta), target),
            [(source(to_t[d]), target, (to_t[d], gx, gy)) for d in range(1, A)],
            t_send, t_recv,
        )

    def along_y(it, way, c, source, target):
        return exchange(
            it, way, c, (source(gy), target),
            [(source(to_y[d]), target, (ta, gx, to_y[d])) for d in range(1, B)],
            y_send, y_recv,
        )

    def landed(pair):
        pair[0].wait()
        for copy in pair[1]:
            copy.wait_recv()

    def sent(pairs):
        for pair in pairs:
            for copy in pair[1]:
                copy.wait_send()

    def place(i):
        return (i + piece - 1) % piece

    ends = [ROWS * (j + 1) - 1 for j in range(stages - 1)] + [piece]
    cuts = list(zip([0] + ends[:-1], ends))

    halo = [
        remote(pot_in.at[0], ht.at[0], halo_send.at[0, 0], halo_recv.at[0, 0], (to_t[A - 1], gx, gy)),
        remote(pot.at[0, 0], pot.at[0, X], halo_send.at[0, 1], halo_recv.at[0, 1], (ta, to_x[G - 1], gy)),
    ]
    for copy in halo:
        copy.start()
    t_halo, x_halo = [halo[0]], halo[1]
    unsent = []

    for it in range(ITERS):
        y_halo = remote(
            face_p.at[it], hyp.at[it], halo_send.at[it, 2], halo_recv.at[it, 2],
            (ta, gx, to_y[B - 1]),
        )
        y_halo.start()
        if it == 0:
            prepare()
            loads[0].wait()
        for copy in t_halo:
            copy.wait_recv()
        y_halo.wait_recv()

        def project_rows(j):
            def group(a, _):
                n = a * stages + j
                x = n * ROWS
                here = pot[it, pl.ds(x, ROWS), :, :].reshape(high, Y)
                nxt = rows_of([ht[it, pl.ds(x + r, 1), :] for r in range(ROWS)])
                nxt = jnp.where(time == T - 1, nxt, pltpu.roll(here, high - 1, 0))
                edge_t = (time == T - 1) & (ta == A - 1)
                slope_t = jnp.where(edge_t, 0.0, nxt - here)
                nxt = pot[it, pl.ds(x + 1, ROWS), :, :].reshape(high, Y)
                edge_x = (sub >= high - T) & ((n == groups - 1) & (gx == G - 1))
                slope_x = jnp.where(edge_x, 0.0, nxt - here)
                nxt = jnp.where(
                    lane == Y - 1, unpack(hyp[it, pl.ds(n, 1), :]), pltpu.roll(here, Y - 1, 1)
                )
                edge_y = (lane == Y - 1) & (gy == B - 1)
                slope_y = jnp.where(edge_y, 0.0, nxt - here)
                if it == 0:
                    m = [
                        jnp.concatenate(
                            [middle(momv.at[b], x + r) for r in range(ROWS)], axis=0
                        )
                        for b in range(3)
                    ]
                else:
                    m = [momx[b, pl.ds(x, ROWS), :, :].reshape(high, Y) for b in range(3)]
                q = project(slope_t + m[0], slope_x + m[1], slope_y + m[2])
                m = [old + (s - new) for old, s, new in zip(m, (slope_t, slope_x, slope_y), q)]
                for b in range(3):
                    if it == ITERS - 1:
                        for r in range(ROWS):
                            set_middle(momv.at[b], x + r, m[b][r * T : (r + 1) * T])
                    else:
                        momx[b, pl.ds(x, ROWS), :, :] = m[b].reshape(ROWS, T, Y)
                wt = jnp.where(edge_t, 0.0, m[0] - q[0])
                wx = jnp.where(edge_x, 0.0, m[1] - q[1])
                wy = jnp.where(edge_y, 0.0, m[2] - q[2])
                for r in range(ROWS):
                    face_t[j, pl.ds(a * ROWS + r, 1), :] = wt[(r + 1) * T - 1 : (r + 1) * T]
                face_y[j, pl.ds(a, 1), :] = pack(wy[:, Y - 1 : Y])
                wx_all[pl.ds(x, ROWS), :, :] = wx.reshape(ROWS, T, Y)
                last = rows_of([rho_end[pl.ds(x + r, 1), :] for r in range(ROWS)])
                begin = rows_of([rho_start[pl.ds(x + r, 1), :] for r in range(ROWS)])
                bound = jnp.where(edge_t, last, 0.0) - jnp.where(
                    (time == 0) & (ta == 0), begin, 0.0
                )
                wt_back = jnp.where(time == 0, 0.0, pltpu.roll(wt, 1, 0))
                wy_back = jnp.where(lane == 0, 0.0, pltpu.roll(wy, 1, 1))
                value = wt - wt_back + wx + (wy - wy_back) + bound
                for r in range(ROWS):
                    src[a, place(j * ROWS + r)] = value[r * T : (r + 1) * T]
                return 0

            lax.fori_loop(0, A, group, 0)

        def send_faces(j):
            copies = [
                remote(face_t.at[j], hwt.at[it, j], w_send.at[it, j, 0], w_recv.at[it, j, 0], (to_t[1], gx, gy)),
                remote(face_y.at[j], hwy.at[it, j], w_send.at[it, j, 1], w_recv.at[it, j, 1], (ta, gx, to_y[1])),
            ]
            for copy in copies:
                copy.start()
            return copies

        def finish_rows(j):
            def group(a, _):
                x = (a * stages + j) * ROWS
                before = unpack(hwy[it, j, pl.ds(a, 1), :])
                before = jnp.where((lane == 0) & (gy > 0), before, 0.0)
                early = rows_of([hwt[it, j, pl.ds(a * ROWS + r, 1), :] for r in range(ROWS)])
                before = before + jnp.where((time == 0) & (ta > 0), early, 0.0)
                for r in range(ROWS):
                    value = src[a, place(j * ROWS + r)] - before[r * T : (r + 1) * T]
                    if j + r:
                        value = value - wx_all[x + r - 1]
                    src[a, place(j * ROWS + r)] = value
                return 0

            lax.fori_loop(0, A, group, 0)

        faces, t_out = [], []

        def close_stage(j):
            for copy in faces[j]:
                copy.wait_recv()
            finish_rows(j)
            if j == stages - 1:
                wx_halo.wait_recv()
                src[0, place(0)] = src[0, place(0)] - jnp.where(gx > 0, hwx[it], 0.0)
                for a in range(1, A):
                    src[a, place(0)] = src[a, place(0)] - wx_all[a * piece - 1]
            lo, hi = cuts[j]
            t_out.append(
                along_t(
                    it, 0, j,
                    lambda other: src.at[other, pl.ds(lo, hi - lo), :, :],
                    r1.at[it, pl.ds(lo, hi - lo), pl.ds(ta * T, T), :],
                )
            )

        for j in range(stages):
            if j == stages - 1:
                x_halo.wait_recv()
            project_rows(j)
            faces.append(send_faces(j))
            if j == stages - 1:
                wx_halo = remote(
                    wx_all.at[X - 1], hwx.at[it], halo_send.at[it, 3], halo_recv.at[it, 3],
                    (ta, to_x[1], gy),
                )
                wx_halo.start()
            if j:
                close_stage(j - 1)
        close_stage(stages - 1)
        if it == ITERS - 1:
            store = pltpu.make_async_copy(momv, mom_out, load_sem.at[0])
            store.start()
        sent(unsent)
        if it == 0:
            loads[1].wait()
            loads[2].wait()

        y_out = []
        half = cuts[stages // 2 - 1][1] if stages > 1 else piece
        for j, (lo, hi) in enumerate(cuts):
            landed(t_out[j])
            for a in range(lo, hi, 2):
                some = range(a, min(a + 2, hi))
                wide = jnp.concatenate([r1[it, p] for p in some], axis=1)
                wide = table_left(ct, wide)
                for n, p in enumerate(some):
                    s2[p] = wide[:, n * Y : (n + 1) * Y]
            y_out.append(
                along_y(
                    it, 1, j,
                    lambda other: s2.at[pl.ds(lo, hi - lo), pl.ds(other * KT, KT), :],
                    r2.at[it, pl.ds(lo, hi - lo), :, pl.ds(pl.multiple_of(gy * Y, Y), Y)],
                )
            )

        def forward_y(lo, hi):
            for j in range(stages):
                if lo < cuts[j][1] <= hi:
                    landed(y_out[j])
            value = r2[it, pl.ds(lo, hi - lo), :, :].reshape((hi - lo) * KT, NY)
            value = table_right(value, cyt)
            sp[pl.ds(lo, hi - lo)] = value.reshape(hi - lo, KT, NY)

        forward_y(0, half)
        if half < piece:
            forward_y(half, piece)

        def forward(j, _):
            lanes = pl.ds(pl.multiple_of(j * 128, 128), 128)
            value = sp[place(0), :, lanes]
            left = jnp.zeros_like(value)
            for i in range(piece - 1):
                left = left + cg[i, :, lanes] * value
                value = sp[place(i + 1), :, lanes] + ci[i, :, lanes] * value
                sp[place(i + 1), :, lanes] = value
            for q in range(KT // 4):
                part = slice(8 * (q // 2), 8 * (q // 2) + 8)
                a, b = left[part], value[part]
                if q % 2:
                    tile = jnp.where(low, pltpu.roll(a, 4, 0), b)
                else:
                    tile = jnp.where(low, a, pltpu.roll(b, 4, 0))
                fwd_out[q * B + j] = tile
            return 0

        inner_sum = jnp.zeros((8, 128), jnp.float32)
        for i in range(piece - 1):
            begin = 0.5 * (piece * (piece - 1) - i * (i + 1))
            other = 0.5 * (i + 1) * (piece - 1 - i)
            inner_sum = inner_sum + jnp.where(me == 0, begin, other) * sp[place(i), 0:8, 0:128]
        extra_out[0] = inner_sum
        lax.fori_loop(0, NY // 128, forward, 0)

        def scatter(phase, outgoing, incoming):
            copies = [
                remote(
                    outgoing.at[to_x[dx] * A + to_t[dt]], incoming.at[it, me],
                    p_send.at[it, phase, n], p_recv.at[it, phase, n],
                    (to_t[dt], to_x[dx], gy),
                )
                for n, (dx, dt) in enumerate(partners)
            ]
            for copy in copies:
                copy.start()
            incoming[it, me] = outgoing[me]
            return copies

        def gather_copy(k):
            return remote(
                extra_out.at[0], extra_in.at[it, k], e_send.at[it, k], e_recv.at[it, k],
                (0, 0, gy),
            )

        def spread_copy(k):
            return remote(
                extra_out.at[1], extra_in.at[it, pieces], e_send.at[it, k], e_recv.at[it, pieces],
                (lax.rem(k, A), k // A, gy),
            )

        head = (gy == 0) & (me == 0)
        tail = (gy == 0) & (me > 0)
        gathers = scatter(0, fwd_out, fwd_in)

        @pl.when(tail)
        def _():
            gather_copy(me).start()

        @pl.when(head)
        def _():
            extra_in[it, 0] = extra_out[0]

            @pl.loop(1, pieces)
            def _(k):
                gather_copy(k).wait_recv()

        for copy in gathers:
            copy.wait_recv()

        value = fwd_in[it, 0] + pltpu.roll(fwd_in[it, 1], 4, 0)
        before = [value]
        for j in range(1, pieces):
            given = fwd_in[it, j]
            if j + 1 < pieces:
                given = given + pltpu.roll(fwd_in[it, j + 1], 4, 0)
            value = given + rra[j - 1] * value
            before.append(value)
        full = value
        value = rip[pieces - 1] * value
        weighted = value * (0.5 * (piece + 1))
        for j in range(pieces - 2, -1, -1):
            here = rip[j] * before[j] + rra[j] * value
            back_out[j + 1] = jnp.where(low, pltpu.roll(here, 4, 0), value)
            value = here
            weighted = weighted + value * (
                piece + 0.5 * (piece - 1) if j == 0 else 1.0 * piece
            )
        back_out[0] = jnp.where(low, 0.0, value)
        returns = scatter(1, back_out, back_in)

        @pl.when(head)
        def _():
            total = lax.fori_loop(
                1, pieces, lambda k, acc: acc + extra_in[it, k], extra_in[it, 0]
            )
            excess = pltpu.roll(full, 4, 0)
            level = -(total + pltpu.roll(weighted, 4, 0)) / NX - excess * (
                (NX * NX - 1.0) / (6.0 * NX)
            )
            row = lax.broadcasted_iota(jnp.int32, (8, 128), 0)
            extra_out[1] = jnp.where(row == 0, excess, pltpu.roll(level, 1, 0))
            extra_in[it, pieces] = extra_out[1]

            @pl.loop(1, pieces)
            def _(k):
                spread_copy(k).start()

        if it == 0:
            loads[3].wait()
            loads[4].wait()
        for copy in returns:
            copy.wait_recv()

        @pl.when(tail)
        def _():
            spread_copy(me).wait_recv()

        def backward(j, _):
            lanes = pl.ds(pl.multiple_of(j * 128, 128), 128)
            left, value = [], []
            for n in range(KT // 8):
                a = back_in[it, 2 * n * B + j]
                b = back_in[it, (2 * n + 1) * B + j]
                left.append(jnp.where(low, a, pltpu.roll(b, 4, 0)))
                value.append(jnp.where(low, pltpu.roll(a, 4, 0), b))
            left = jnp.concatenate(left, axis=0)
            value = jnp.concatenate(value, axis=0)
            sq[piece - 1, :, lanes] = value
            for i in range(piece - 2, -1, -1):
                value = (
                    ci[i, :, lanes] * (sp[place(i), :, lanes] + value)
                    + cg[i, :, lanes] * left
                )
                sq[i, :, lanes] = value
            return 0

        lax.fori_loop(0, NY // 128, backward, 0)

        @pl.when(gy == 0)
        def _():
            row = lax.broadcasted_iota(jnp.int32, (8, 128), 0)
            constant = (row == 0) & (lax.broadcasted_iota(jnp.int32, (8, 128), 1) == 0)
            excess = extra_in[it, pieces]
            level = pltpu.roll(excess, 7, 0)
            for i in range(piece):
                cell = (me * piece + i).astype(jnp.float32)
                ramp = cell * (cell + 1.0) * (0.5 / NX)
                sq[i, 0:8, 0:128] += jnp.where(constant, excess * ramp + level, 0.0)

        y_back, t_back = [], []
        parts = 2 if stages % 2 == 0 else 1
        for n in range(parts):
            count = piece // parts
            lines = pl.ds(n * count, count)
            value = table_right(sq[lines].reshape(count * KT, NY), cy)
            s3[lines] = value.reshape(count, KT, NY)
            for j in range(n * stages // parts, (n + 1) * stages // parts):
                y_back.append(
                    along_y(
                        it, 3, j,
                        lambda other: s3.at[
                            pl.ds(j * ROWS, ROWS), :, pl.ds(pl.multiple_of(other * Y, Y), Y)
                        ],
                        r3.at[it, pl.ds(j * ROWS, ROWS), pl.ds(gy * KT, KT), :],
                    )
                )
        more = it + 1 < ITERS

        def x_copy(d):
            return remote(
                s4.at[0, pl.ds(d * T, T), :], pot.at[it + 1, X],
                xh_send.at[it, d], xh_recv.at[it], (d, to_x[G - 1], gy),
            )

        for j in range(stages):
            landed(y_back[j])
            for x in range(j * ROWS, (j + 1) * ROWS, 2):
                wide = jnp.concatenate([r3[it, x], r3[it, x + 1]], axis=1)
                wide = table_left(ctt, wide)
                for n in range(2):
                    value = wide[:, n * Y : (n + 1) * Y]
                    s4[x + n] = value
                    if more:
                        for d in range(A):
                            t = (d + 1) * T % NT
                            ht_out[d, x + n : x + n + 1, :] = value[t : t + 1]
            if more and j == stages - 1:
                ht[it + 1, pl.ds(ta * piece, piece), :] = ht_out[ta]
                t_halo = [
                    remote(
                        ht_out.at[to_t[d]], ht.at[it + 1, pl.ds(ta * piece, piece), :],
                        th_send.at[it, d - 1], th_recv.at[it, d - 1], (to_t[d], gx, gy),
                    )
                    for d in range(1, A)
                ]
                for copy in t_halo:
                    copy.start()
            t_back.append(
                along_t(
                    it, 2, j,
                    lambda other: s4.at[pl.ds(j * ROWS, ROWS), pl.ds(other * T, T), :],
                    pot.at[it + 1, pl.ds(ta * piece + j * ROWS, ROWS), :, :],
                )
            )
            if more and j == 0:

                @pl.when(ta == 0)
                def _():
                    for d in range(A):
                        x_copy(d).start()

        for j in range(stages):
            landed(t_back[j])

            def arrived(a, _):
                n = a * stages + j
                if more:
                    pack_first(it + 1, n)
                else:
                    for r in range(ROWS):
                        set_middle(pot_out, n * ROWS + r, pot[it + 1, n * ROWS + r])
                return 0

            lax.fori_loop(0, A, arrived, 0)

        if it == 0:
            for copy in halo:
                copy.wait_send()
        y_halo.wait_send()
        wx_halo.wait_send()
        for copies in faces:
            for copy in copies:
                copy.wait_send()
        sent(t_out + y_out + y_back)
        for copy in gathers + returns:
            copy.wait_send()

        @pl.when(tail)
        def _():
            gather_copy(me).wait_send()

        @pl.when(head)
        def _():
            @pl.loop(1, pieces)
            def _(k):
                spread_copy(k).wait_send()

        sent(t_back)
        if more:
            x_halo = x_copy(0)
            for copy in t_halo:
                copy.wait_send()

            @pl.when(ta == 0)
            def _():
                for d in range(A):
                    x_copy(d).wait_send()

    store.wait()


def parts_of(table):
    parts, rest = [], np.asarray(table, np.float64)
    for _ in range(3):
        part = rest.astype(np.float32).astype(jnp.bfloat16)
        parts.append(part)
        rest = rest - part.astype(np.float64)
    return np.stack(parts)


def on_device(sizes, momenta, potential, rho_start, rho_end):
    A, G, B, T, X, Y = sizes
    piece, KT, pieces = X // A, NT // B, G * A
    stages, groups = piece // ROWS, X // ROWS
    assert Y == 128 and ROWS * T <= 128 and T % 8 == 0 and piece % ROWS == 0
    assert KT % 8 == 0 and pieces == (KT // 4) * B and ITERS > 1
    table_t, table_y = parts_of(cosine_table(NT)), parts_of(cosine_table(NY))
    turned_t, turned_y = parts_of(cosine_table(NT).T), parts_of(cosine_table(NY).T)
    e_t = eigenvalue(NT)
    spread_t = np.broadcast_to(e_t[:, None], (NT, 128)).astype(np.float32)
    spread_8 = np.broadcast_to(
        np.concatenate([e_t.reshape(NT // 4, 4)] * 2, axis=1)[:, :, None], (NT // 4, 8, 128)
    ).astype(np.float32)
    spread_y = np.broadcast_to(
        eigenvalue(NY).reshape(B, 1, 128), (B, 8, 128)
    ).astype(np.float32)
    tables = [
        table_t.reshape(3 * NT, NT), turned_t.reshape(3 * NT, NT), table_y, turned_y,
        spread_t, spread_8, spread_y,
    ]
    operands = [momenta, potential, rho_start, rho_end] + [
        jnp.asarray(np.ascontiguousarray(table)) for table in tables
    ]
    f32 = jnp.float32
    vmem = pl.BlockSpec(memory_space=pltpu.VMEM)
    hbm = pl.BlockSpec(memory_space=pl.ANY)
    dma = pltpu.SemaphoreType.DMA
    tall = max(groups, 8)

    def held(*shape, dtype=f32):
        return pltpu.VMEM(shape, dtype)

    return pl.pallas_call(
        functools.partial(kernel, sizes),
        out_shape=(
            jax.ShapeDtypeStruct(momenta.shape, f32),
            jax.ShapeDtypeStruct(potential.shape, f32),
        ),
        in_specs=[hbm, vmem, vmem, vmem, hbm, hbm, hbm, hbm, vmem, vmem, vmem],
        out_specs=(hbm, vmem),
        scratch_shapes=[
            held(3, T, X, Y),
            held(3, X, T, Y),
            held(3 * NT, NT, dtype=jnp.bfloat16),
            held(3 * NT, NT, dtype=jnp.bfloat16),
            held(3, NY, NY, dtype=jnp.bfloat16),
            held(3, NY, NY, dtype=jnp.bfloat16),
            held(ITERS + 1, X + 1, T, Y),
            held(ITERS, X, Y),
            held(ITERS, tall, Y),
            held(ITERS, stages, A * ROWS, Y),
            held(ITERS, T, Y),
            held(ITERS, stages, 8, Y),
            held(ITERS, tall, Y),
            held(stages, A * ROWS, Y),
            held(stages, 8, Y),
            held(A, piece, Y),
            held(X, T, Y),
            held(A, piece, T, Y),
            held(ITERS, piece, NT, Y),
            held(piece, NT, Y),
            held(ITERS, piece, KT, NY),
            held(piece, KT, NY),
            held(piece, KT, NY),
            held(piece, KT, NY),
            held(ITERS, piece, NT, Y),
            held(piece, NT, Y),
            held(piece, KT, NY),
            held(piece, KT, NY),
            held(pieces, 8, 128),
            held(pieces, 8, 128),
            held(pieces, 8, 128),
            held(ITERS, pieces, 8, 128),
            held(pieces, 8, 128),
            held(ITERS, pieces, 8, 128),
            held(2, 8, 128),
            held(ITERS, pieces + 1, 8, 128),
            dma((5,)),
            dma((ITERS, 4)),
            dma((ITERS, 4)),
            dma((ITERS, stages, 2)),
            dma((ITERS, stages, 2)),
            dma((ITERS, A - 1)),
            dma((ITERS, A - 1)),
            dma((ITERS, A)),
            dma((ITERS,)),
            dma((ITERS, 2, stages, A - 1)),
            dma((ITERS, 2, stages, A - 1)),
            dma((ITERS, 2, stages, B - 1)),
            dma((ITERS, 2, stages, B - 1)),
            dma((ITERS, 2, pieces - 1)),
            dma((ITERS, 2, pieces - 1)),
            dma((ITERS, pieces)),
            dma((ITERS, pieces + 1)),
            dma((ITERS, 4, stages)),
        ],
        compiler_params=pltpu.CompilerParams(
            collective_id=0, has_side_effects=True, vmem_limit_bytes=60 << 20
        ),
    )(*operands)


def solution(mesh):
    A, G, B = (mesh.shape[name] for name in ("ta", "gx", "gy"))
    sizes = (A, G, B, NT // A, NX // G, NY // B)
    placed = (P(None, "ta", "gx", "gy"), P("ta", "gx", "gy"), P("gx", "gy"), P("gx", "gy"))
    return jax.shard_map(
        functools.partial(on_device, sizes),
        mesh=mesh,
        in_specs=placed,
        out_specs=(P(None, "ta", "gx", "gy"), P("ta", "gx", "gy")),
        check_vma=False,
    )
```

```python
import functools

import jax
import jax.numpy as jnp
import numpy as np
from jax import lax
from jax.experimental import pallas as pl
from jax.experimental.pallas import tpu as pltpu
from jax.sharding import PartitionSpec as P

NT = 128
NX = 512
NY = 1024
ITERS = 2
NEWTON = 8
ROWS = 4

MESH = pl.DeviceIdType.MESH


def cosine_table(count):
    modes = np.arange(count, dtype=np.int64)[:, None]
    cells = np.arange(count, dtype=np.int64)[None, :]
    phase = modes * (2 * cells + 1) % (4 * count)
    weight = np.where(modes == 0, 1.0, 2.0) / count
    return np.sqrt(weight) * np.cos(phase * (np.pi / (2 * count)))


def eigenvalue(count):
    return (2.0 * np.sin(np.arange(count) * (np.pi / (2 * count)))) ** 2


def split(value):
    parts = []
    for _ in range(3):
        part = value.astype(jnp.bfloat16)
        parts.append(part)
        value = value - part.astype(jnp.float32)
    return parts


def product(left, right):
    return jnp.dot(left, right, preferred_element_type=jnp.float32)


def table_right(value, table):
    rows = value.shape[0]
    parts = split(value)
    total = product(parts[0], table[2])
    middle_ = product(jnp.concatenate(parts[:2], axis=0), table[1])
    large = product(jnp.concatenate(parts, axis=0), table[0])
    total = total + (middle_[rows:] + large[2 * rows :])
    total = total + (middle_[:rows] + large[rows : 2 * rows])
    return total + large[:rows]


def table_left(table, value):
    rows = table.shape[0] // 3
    parts = split(value)
    total = product(table[:rows], parts[2])
    middle_ = product(table[: 2 * rows], parts[1])
    large = product(table[...], parts[0])
    total = total + (middle_[rows:] + large[2 * rows :])
    total = total + (middle_[:rows] + large[rows : 2 * rows])
    return total + large[:rows]


def middle(ref, index):
    rows, group, lanes = ref.shape
    return ref.reshape(rows * group, lanes)[pl.ds(index, rows, stride=group), :]


def set_middle(ref, index, value):
    rows, group, lanes = ref.shape
    ref.reshape(rows * group, lanes)[pl.ds(index, rows, stride=group), :] = value


def project(p0, p1, p2):
    s = p1 * p1 + p2 * p2
    half = 0.5 * s
    lam = jnp.zeros_like(p0)
    for _ in range(NEWTON):
        growth = 1.0 + lam
        cube = growth * growth * growth
        lam = jnp.maximum(lam + ((p0 - lam) * cube + half * growth) / (cube + s), 0.0)
    inverse = 1.0 / (1.0 + lam)
    return p0 - lam, p1 * inverse, p2 * inverse


def kernel(
    sizes,
    mom_hbm, pot_in, rho_start, rho_end, ct_hbm, ctt_hbm, cy_hbm, cyt_hbm, et, et8, ey8,
    mom_out, pot_out,
    momv, momx, ct, ctt, cy, cyt,
    pot, ht, hyp, hwt, hwx, hwy, face_p, face_t, face_y, ht_out, wx_all, src,
    r1, s2, r2, sp, sq, s3, r3, s4, ci, cg, rip, rra,
    fwd_out, fwd_in, back_out, back_in, extra_out, extra_in,
    load_sem, halo_send, halo_recv, yh_send, yh_recv, w_send, w_recv, wx_send, wx_recv,
    th_send, th_recv, xh_send, xh_recv,
    t_send, t_recv, y_send, y_recv, p_send, p_recv, e_send, e_recv, local_sem,
):
    A, G, B, T, X, Y = sizes
    piece = X // A
    KT = NT // B
    pieces = G * A
    stages = piece // ROWS
    groups = X // ROWS
    high = ROWS * T
    ta, gx, gy = (lax.axis_index(name) for name in ("ta", "gx", "gy"))
    me = gx * A + ta
    to_t = [lax.rem(ta + d, A) for d in range(A)]
    to_x = [lax.rem(gx + d, G) for d in range(G)]
    to_y = [lax.rem(gy + d, B) for d in range(B)]
    partners = sorted(
        ((dx, dt) for dx in range(G) for dt in range(A) if dx or dt),
        key=lambda p: -(4 * (p[0] % 2) + min(p[0], G - p[0]) + min(p[1], A - p[1])),
    )

    def remote(source, target, send, recv, where):
        return pltpu.make_async_remote_copy(
            src_ref=source, dst_ref=target, send_sem=send, recv_sem=recv,
            device_id=where, device_id_type=MESH,
        )

    loads = [
        pltpu.make_async_copy(source, target, load_sem.at[n])
        for n, (source, target) in enumerate(
            ((mom_hbm, momv), (ct_hbm, ct), (cyt_hbm, cyt), (cy_hbm, cy), (ctt_hbm, ctt))
        )
    ]
    for load in loads:
        load.start()

    barrier = pltpu.get_barrier_semaphore()
    for dx, dt in partners:
        pl.semaphore_signal(
            barrier, inc=1, device_id=(to_t[dt], to_x[dx], gy), device_id_type=MESH
        )
    for d in range(1, B):
        pl.semaphore_signal(
            barrier, inc=1, device_id=(ta, gx, to_y[d]), device_id_type=MESH
        )

    sub = lax.broadcasted_iota(jnp.int32, (high, Y), 0)
    lane = lax.broadcasted_iota(jnp.int32, (high, Y), 1)
    eye = sub == lane
    time = lax.rem(sub, T)
    low = lax.broadcasted_iota(jnp.int32, (8, 128), 0) < 4

    def pack(column):
        spread = jnp.broadcast_to(column, (high, Y))
        return jnp.sum(jnp.where(eye, spread, 0.0), axis=0, keepdims=True)

    def unpack(row):
        spread = jnp.broadcast_to(row, (high, Y))
        return jnp.sum(jnp.where(eye, spread, 0.0), axis=1, keepdims=True)

    def rows_of(parts):
        return jnp.concatenate([jnp.broadcast_to(p, (T, Y)) for p in parts], axis=0)

    def pack_first(it, j):
        def group(a, _):
            x = (a * stages + j) * ROWS
            value = pot[it, pl.ds(x, ROWS), :, :].reshape(high, Y)
            face_p[it, j, pl.ds(a, 1), :] = pack(value[:, 0:1])
            return 0

        lax.fori_loop(0, A, group, 0)

    def first(a, _):
        for j in range(stages):
            for r in range(ROWS):
                x = (a * stages + j) * ROWS + r
                pot[0, x] = middle(pot_in, x)
                ht_out[j, a, r : r + 1, :] = pot_in[0, pl.ds(x, 1), :]
        return 0

    lax.fori_loop(0, A, first, 0)
    for j in range(stages):
        pack_first(0, j)
    pl.semaphore_wait(barrier, pieces + B - 2)

    def prepare():
        def coefficients(j, _):
            sigma = et[pl.ds(gy * KT, KT), :] + ey8[j][0:1, :]
            lanes = pl.ds(pl.multiple_of(j * 128, 128), 128)
            g = jnp.where(me == 0, 0.0, jnp.ones_like(sigma))
            h = sigma
            for i in range(piece - 1):
                inv = 1.0 / (g + 1.0 + h)
                g = g * inv
                ci[i, :, lanes] = inv
                cg[i, :, lanes] = g
                h = sigma + h * inv
            return 0

        lax.fori_loop(0, NY // 128, coefficients, 0)

        sigma = et8[gy * (KT // 4) + me // B] + ey8[lax.rem(me, B)]
        one = jnp.ones_like(sigma)

        def inner(i, state):
            g, h, h_first, ground = state
            inv = 1.0 / (g + 1.0 + h)
            inv_first = 1.0 / (1.0 + h_first)
            return (
                g * inv, sigma + h * inv, sigma + h_first * inv_first, ground + g * h * inv
            )

        link, h_end, h_first, ground = lax.fori_loop(
            0, piece - 1, inner, (one, sigma, sigma, jnp.zeros_like(sigma))
        )

        def outer(j, s):
            inv = 1.0 / (s + link)
            rip[j] = inv
            rra[j] = link * inv
            return jnp.where(j == pieces - 2, h_end, h_end + ground) + link * s * inv

        s_last = lax.fori_loop(0, pieces - 1, outer, h_first + ground)
        rip[pieces - 1] = jnp.where(
            s_last > 0.0, 1.0 / jnp.where(s_last > 0.0, s_last, 1.0), 0.0
        )

    def exchange(it, way, c, own, others, sends, recvs):
        local = pltpu.make_async_copy(*own, local_sem.at[it, way, c])
        local.start()
        copies = [
            remote(source, target, sends.at[it, way // 2, c, k], recvs.at[it, way // 2, c, k], where)
            for k, (source, target, where) in enumerate(others)
        ]
        for copy in copies:
            copy.start()
        return local, copies

    def along_t(it, way, c, source, target):
        return exchange(
            it, way, c, (source(ta), target),
            [(source(to_t[d]), target, (to_t[d], gx, gy)) for d in range(1, A)],
            t_send, t_recv,
        )

    def along_y(it, way, c, source, target):
        return exchange(
            it, way, c, (source(gy), target),
            [(source(to_y[d]), target, (ta, gx, to_y[d])) for d in range(1, B)],
            y_send, y_recv,
        )

    def landed(pair):
        pair[0].wait()
        for copy in pair[1]:
            copy.wait_recv()

    def sent(pairs):
        for pair in pairs:
            for copy in pair[1]:
                copy.wait_send()

    def place(i):
        return (i + piece - 1) % piece

    done = [ROWS * (j + 1) - 1 for j in range(stages)]
    cuts = [(j, ROWS * j - 1 if j else 0, done[j]) for j in range(stages - 1)]
    cuts += [(stages - 1, ROWS * (stages - 1) - 1, piece - 2), (stages - 1, piece - 2, piece)]
    marks = [0, 2] + list(range(5, piece, 3))[: 2 if stages > 2 else 0]
    marks += list(range(marks[-1] + ROWS, piece, ROWS)) + [piece]
    backs = list(zip(marks[:-1], marks[1:]))

    def y_face(it, j):
        return remote(
            face_p.at[it, j], hyp.at[it, j], yh_send.at[it, j], yh_recv.at[it, j],
            (ta, gx, to_y[B - 1]),
        )

    def t_face(it, j, d):
        return remote(
            ht_out.at[j, to_t[d]], ht.at[it + 1, j, ta], th_send.at[it, j, d - 1],
            th_recv.at[it, j, d - 1], (to_t[d], gx, gy),
        )

    def x_face(it, d):
        return remote(
            s4.at[0, pl.ds(d * T, T), :], pot.at[it + 1, X],
            xh_send.at[it, d], xh_recv.at[it], (d, to_x[G - 1], gy),
        )

    def wx_face(it):
        return remote(
            wx_all.at[X - 1], hwx.at[it], wx_send.at[it], wx_recv.at[it], (ta, to_x[1], gy)
        )

    halo = [
        remote(ht_out, ht.at[0], halo_send.at[0], halo_recv.at[0], (to_t[A - 1], gx, gy)),
        remote(pot.at[0, 0], pot.at[0, X], halo_send.at[1], halo_recv.at[1], (ta, to_x[G - 1], gy)),
    ]
    for j in range(stages):
        y_face(0, j).start()
    for copy in halo:
        copy.start()
    faces = [[] for _ in range(ITERS)]
    t_out = [[] for _ in range(ITERS)]
    unsent = []

    def project_rows(it, j):
        def group(a, _):
            n = a * stages + j
            x = n * ROWS
            here = pot[it, pl.ds(x, ROWS), :, :].reshape(high, Y)
            nxt = rows_of([ht[it, j, a, r : r + 1, :] for r in range(ROWS)])
            nxt = jnp.where(time == T - 1, nxt, pltpu.roll(here, high - 1, 0))
            edge_t = (time == T - 1) & (ta == A - 1)
            slope_t = jnp.where(edge_t, 0.0, nxt - here)
            nxt = pot[it, pl.ds(x + 1, ROWS), :, :].reshape(high, Y)
            edge_x = (sub >= high - T) & ((n == groups - 1) & (gx == G - 1))
            slope_x = jnp.where(edge_x, 0.0, nxt - here)
            nxt = jnp.where(
                lane == Y - 1, unpack(hyp[it, j, pl.ds(a, 1), :]), pltpu.roll(here, Y - 1, 1)
            )
            edge_y = (lane == Y - 1) & (gy == B - 1)
            slope_y = jnp.where(edge_y, 0.0, nxt - here)
            if it == 0:
                m = [
                    jnp.concatenate(
                        [middle(momv.at[b], x + r) for r in range(ROWS)], axis=0
                    )
                    for b in range(3)
                ]
            else:
                m = [momx[b, pl.ds(x, ROWS), :, :].reshape(high, Y) for b in range(3)]
            q = project(slope_t + m[0], slope_x + m[1], slope_y + m[2])
            m = [old + (s - new) for old, s, new in zip(m, (slope_t, slope_x, slope_y), q)]
            for b in range(3):
                if it == ITERS - 1:
                    for r in range(ROWS):
                        set_middle(momv.at[b], x + r, m[b][r * T : (r + 1) * T])
                else:
                    momx[b, pl.ds(x, ROWS), :, :] = m[b].reshape(ROWS, T, Y)
            wt = jnp.where(edge_t, 0.0, m[0] - q[0])
            wx = jnp.where(edge_x, 0.0, m[1] - q[1])
            wy = jnp.where(edge_y, 0.0, m[2] - q[2])
            for r in range(ROWS):
                face_t[j, pl.ds(a * ROWS + r, 1), :] = wt[(r + 1) * T - 1 : (r + 1) * T]
            face_y[j, pl.ds(a, 1), :] = pack(wy[:, Y - 1 : Y])
            wx_all[pl.ds(x, ROWS), :, :] = wx.reshape(ROWS, T, Y)
            last = rows_of([rho_end[pl.ds(x + r, 1), :] for r in range(ROWS)])
            begin = rows_of([rho_start[pl.ds(x + r, 1), :] for r in range(ROWS)])
            bound = jnp.where(edge_t, last, 0.0) - jnp.where(
                (time == 0) & (ta == 0), begin, 0.0
            )
            wt_back = jnp.where(time == 0, 0.0, pltpu.roll(wt, 1, 0))
            wy_back = jnp.where(lane == 0, 0.0, pltpu.roll(wy, 1, 1))
            value = wt - wt_back + wx + (wy - wy_back) + bound
            for r in range(ROWS):
                src[a, place(j * ROWS + r)] = value[r * T : (r + 1) * T]
            return 0

        lax.fori_loop(0, A, group, 0)

    def send_faces(it, j):
        copies = [
            remote(face_t.at[j], hwt.at[it, j], w_send.at[it, j, 0], w_recv.at[it, j, 0], (to_t[1], gx, gy)),
            remote(face_y.at[j], hwy.at[it, j], w_send.at[it, j, 1], w_recv.at[it, j, 1], (ta, gx, to_y[1])),
        ]
        for copy in copies:
            copy.start()
        return copies

    def finish_rows(it, j):
        def group(a, _):
            x = (a * stages + j) * ROWS
            before = unpack(hwy[it, j, pl.ds(a, 1), :])
            before = jnp.where((lane == 0) & (gy > 0), before, 0.0)
            early = rows_of([hwt[it, j, pl.ds(a * ROWS + r, 1), :] for r in range(ROWS)])
            before = before + jnp.where((time == 0) & (ta > 0), early, 0.0)
            for r in range(ROWS):
                value = src[a, place(j * ROWS + r)] - before[r * T : (r + 1) * T]
                if j + r:
                    value = value - wx_all[x + r - 1]
                src[a, place(j * ROWS + r)] = value
            return 0

        lax.fori_loop(0, A, group, 0)

    def close_stage(it, j):
        for copy in faces[it][j]:
            copy.wait_recv()
        finish_rows(it, j)
        if j == stages - 1:
            wx_face(it).wait_recv()
            src[0, place(0)] = src[0, place(0)] - jnp.where(gx > 0, hwx[it], 0.0)
            for a in range(1, A):
                src[a, place(0)] = src[a, place(0)] - wx_all[a * piece - 1]
        for c, (stage, lo, hi) in enumerate(cuts):
            if stage == j:
                t_out[it].append(
                    along_t(
                        it, 0, c,
                        lambda other: src.at[other, pl.ds(lo, hi - lo), :, :],
                        r1.at[it, pl.ds(lo, hi - lo), pl.ds(ta * T, T), :],
                    )
                )

    def run_stage(it, j):
        if it:
            for d in range(1, A):
                t_face(it - 1, j, d).wait_recv()
        y_face(it, j).wait_recv()
        if j == stages - 1:
            if it:
                x_face(it - 1, 0).wait_recv()
            else:
                halo[1].wait_recv()
        project_rows(it, j)
        faces[it].append(send_faces(it, j))
        if j == stages - 1:
            wx_face(it).start()
        if j:
            close_stage(it, j - 1)
        if j == stages - 1:
            close_stage(it, j)

    loads[0].wait()
    halo[0].wait_recv()
    for j in range(stages):
        run_stage(0, j)
    prepare()
    loads[1].wait()
    loads[2].wait()
    for copy in halo:
        copy.wait_send()

    for it in range(ITERS):
        if it == ITERS - 1:
            store = pltpu.make_async_copy(momv, mom_out, load_sem.at[0])
            store.start()

        y_out = []
        for c, (_, lo, hi) in enumerate(cuts):
            landed(t_out[it][c])
            for a in range(lo, hi, 2):
                some = range(a, min(a + 2, hi))
                wide = jnp.concatenate([r1[it, p] for p in some], axis=1)
                wide = table_left(ct, wide)
                for n, p in enumerate(some):
                    s2[p] = wide[:, n * Y : (n + 1) * Y]
            y_out.append(
                along_y(
                    it, 1, c,
                    lambda other: s2.at[pl.ds(lo, hi - lo), pl.ds(other * KT, KT), :],
                    r2.at[it, pl.ds(lo, hi - lo), :, pl.ds(pl.multiple_of(gy * Y, Y), Y)],
                )
            )

        def forward_y(lo, hi):
            for c in range(len(cuts)):
                if lo < cuts[c][2] <= hi:
                    landed(y_out[c])
            value = r2[it, pl.ds(lo, hi - lo), :, :].reshape((hi - lo) * KT, NY)
            value = table_right(value, cyt)
            sp[pl.ds(lo, hi - lo)] = value.reshape(hi - lo, KT, NY)

        bounds = [0, done[max(stages // 2 - 1, 0)], piece - 2, piece]
        for lo, hi in zip(bounds[:-1], bounds[1:]):
            forward_y(lo, hi)

        def forward(j, _):
            lanes = pl.ds(pl.multiple_of(j * 128, 128), 128)
            value = sp[place(0), :, lanes]
            left = jnp.zeros_like(value)
            for i in range(piece - 1):
                left = left + cg[i, :, lanes] * value
                value = sp[place(i + 1), :, lanes] + ci[i, :, lanes] * value
                sp[place(i + 1), :, lanes] = value
            for q in range(KT // 4):
                part = slice(8 * (q // 2), 8 * (q // 2) + 8)
                a, b = left[part], value[part]
                if q % 2:
                    tile = jnp.where(low, pltpu.roll(a, 4, 0), b)
                else:
                    tile = jnp.where(low, a, pltpu.roll(b, 4, 0))
                fwd_out[q * B + j] = tile
            return 0

        inner_sum = jnp.zeros((8, 128), jnp.float32)
        for i in range(piece - 1):
            begin = 0.5 * (piece * (piece - 1) - i * (i + 1))
            other = 0.5 * (i + 1) * (piece - 1 - i)
            inner_sum = inner_sum + jnp.where(me == 0, begin, other) * sp[place(i), 0:8, 0:128]
        extra_out[0] = inner_sum
        lax.fori_loop(0, NY // 128, forward, 0)

        def scatter(phase, outgoing, incoming):
            copies = [
                remote(
                    outgoing.at[to_x[dx] * A + to_t[dt]], incoming.at[it, me],
                    p_send.at[it, phase, n], p_recv.at[it, phase, n],
                    (to_t[dt], to_x[dx], gy),
                )
                for n, (dx, dt) in enumerate(partners)
            ]
            for copy in copies:
                copy.start()
            incoming[it, me] = outgoing[me]
            return copies

        def gather_copy(k):
            return remote(
                extra_out.at[0], extra_in.at[it, k], e_send.at[it, k], e_recv.at[it, k],
                (0, 0, gy),
            )

        def spread_copy(k):
            return remote(
                extra_out.at[1], extra_in.at[it, pieces], e_send.at[it, k], e_recv.at[it, pieces],
                (lax.rem(k, A), k // A, gy),
            )

        head = (gy == 0) & (me == 0)
        tail = (gy == 0) & (me > 0)
        gathers = scatter(0, fwd_out, fwd_in)

        @pl.when(tail)
        def _():
            gather_copy(me).start()

        @pl.when(head)
        def _():
            extra_in[it, 0] = extra_out[0]

            @pl.loop(1, pieces)
            def _(k):
                gather_copy(k).wait_recv()

        for copy in gathers:
            copy.wait_recv()

        value = fwd_in[it, 0] + pltpu.roll(fwd_in[it, 1], 4, 0)
        before = [value]
        for j in range(1, pieces):
            given = fwd_in[it, j]
            if j + 1 < pieces:
                given = given + pltpu.roll(fwd_in[it, j + 1], 4, 0)
            value = given + rra[j - 1] * value
            before.append(value)
        full = value
        value = rip[pieces - 1] * value
        weighted = value * (0.5 * (piece + 1))
        for j in range(pieces - 2, -1, -1):
            here = rip[j] * before[j] + rra[j] * value
            back_out[j + 1] = jnp.where(low, pltpu.roll(here, 4, 0), value)
            value = here
            weighted = weighted + value * (
                piece + 0.5 * (piece - 1) if j == 0 else 1.0 * piece
            )
        back_out[0] = jnp.where(low, 0.0, value)
        returns = scatter(1, back_out, back_in)

        @pl.when(head)
        def _():
            total = lax.fori_loop(
                1, pieces, lambda k, acc: acc + extra_in[it, k], extra_in[it, 0]
            )
            excess = pltpu.roll(full, 4, 0)
            level = -(total + pltpu.roll(weighted, 4, 0)) / NX - excess * (
                (NX * NX - 1.0) / (6.0 * NX)
            )
            row = lax.broadcasted_iota(jnp.int32, (8, 128), 0)
            extra_out[1] = jnp.where(row == 0, excess, pltpu.roll(level, 1, 0))
            extra_in[it, pieces] = extra_out[1]

            @pl.loop(1, pieces)
            def _(k):
                spread_copy(k).start()

        if it == 0:
            loads[3].wait()
            loads[4].wait()
        for copy in returns:
            copy.wait_recv()

        @pl.when(tail)
        def _():
            spread_copy(me).wait_recv()

        def backward(j, _):
            lanes = pl.ds(pl.multiple_of(j * 128, 128), 128)
            left, value = [], []
            for n in range(KT // 8):
                a = back_in[it, 2 * n * B + j]
                b = back_in[it, (2 * n + 1) * B + j]
                left.append(jnp.where(low, a, pltpu.roll(b, 4, 0)))
                value.append(jnp.where(low, pltpu.roll(a, 4, 0), b))
            left = jnp.concatenate(left, axis=0)
            value = jnp.concatenate(value, axis=0)
            sq[piece - 1, :, lanes] = value
            for i in range(piece - 2, -1, -1):
                value = (
                    ci[i, :, lanes] * (sp[place(i), :, lanes] + value)
                    + cg[i, :, lanes] * left
                )
                sq[i, :, lanes] = value
            return 0

        lax.fori_loop(0, NY // 128, backward, 0)

        @pl.when(gy == 0)
        def _():
            row = lax.broadcasted_iota(jnp.int32, (8, 128), 0)
            constant = (row == 0) & (lax.broadcasted_iota(jnp.int32, (8, 128), 1) == 0)
            excess = extra_in[it, pieces]
            level = pltpu.roll(excess, 7, 0)
            for i in range(piece):
                cell = (me * piece + i).astype(jnp.float32)
                ramp = cell * (cell + 1.0) * (0.5 / NX)
                sq[i, 0:8, 0:128] += jnp.where(constant, excess * ramp + level, 0.0)

        y_back, t_back = [], []
        bounds = [0, 2] + ([backs[2][1]] if stages > 2 else []) + [piece]
        for lo, hi in zip(bounds[:-1], bounds[1:]):
            value = table_right(sq[pl.ds(lo, hi - lo)].reshape((hi - lo) * KT, NY), cy)
            s3[pl.ds(lo, hi - lo)] = value.reshape(hi - lo, KT, NY)
            for c, (low_row, high_row) in enumerate(backs):
                if lo <= low_row and high_row <= hi:
                    lines = pl.ds(low_row, high_row - low_row)
                    y_back.append(
                        along_y(
                            it, 3, c,
                            lambda other: s3.at[
                                lines, :, pl.ds(pl.multiple_of(other * Y, Y), Y)
                            ],
                            r3.at[it, lines, pl.ds(gy * KT, KT), :],
                        )
                    )
        more = it + 1 < ITERS
        sent(unsent)
        if it:

            @pl.when(ta == 0)
            def _():
                for d in range(A):
                    x_face(it - 1, d).wait_send()

        for c, (lo, hi) in enumerate(backs):
            landed(y_back[c])
            for x in range(lo, hi, 2):
                some = range(x, min(x + 2, hi))
                wide = jnp.concatenate([r3[it, p] for p in some], axis=1)
                wide = table_left(ctt, wide)
                for n, p in enumerate(some):
                    value = wide[:, n * Y : (n + 1) * Y]
                    s4[p] = value
                    if more:
                        for d in range(A):
                            t = (d + 1) * T % NT
                            r = p % ROWS
                            ht_out[p // ROWS, d, r : r + 1, :] = value[t : t + 1]
            if more:
                for j in range(stages):
                    if lo < ROWS * (j + 1) <= hi:
                        ht[it + 1, j, ta] = ht_out[j, ta]
                        for d in range(1, A):
                            t_face(it, j, d).start()
            t_back.append(
                along_t(
                    it, 2, c,
                    lambda other: s4.at[pl.ds(lo, hi - lo), pl.ds(other * T, T), :],
                    pot.at[it + 1, pl.ds(ta * piece + lo, hi - lo), pl.ds(0, T), :],
                )
            )
            if more and c == 0:

                @pl.when(ta == 0)
                def _():
                    for d in range(A):
                        x_face(it, d).start()

        wx_face(it).wait_send()
        for j in range(stages):
            y_face(it, j).wait_send()
            for copy in faces[it][j]:
                copy.wait_send()
        sent(t_out[it] + y_out + y_back)
        for copy in gathers + returns:
            copy.wait_send()

        @pl.when(tail)
        def _():
            gather_copy(me).wait_send()

        @pl.when(head)
        def _():
            @pl.loop(1, pieces)
            def _(k):
                spread_copy(k).wait_send()

        for c, (lo, hi) in enumerate(backs):
            landed(t_back[c])
            for j in range(stages):
                if lo < ROWS * (j + 1) <= hi:
                    if more:
                        pack_first(it + 1, j)
                        y_face(it + 1, j).start()
                        if j:
                            run_stage(it + 1, j - 1)
                    else:

                        def arrived(a, _):
                            for r in range(ROWS):
                                x = (a * stages + j) * ROWS + r
                                set_middle(pot_out, x, pot[ITERS, x])
                            return 0

                        lax.fori_loop(0, A, arrived, 0)
        if more:
            run_stage(it + 1, stages - 1)
            for j in range(stages):
                for d in range(1, A):
                    t_face(it, j, d).wait_send()
        unsent = t_back
    sent(unsent)
    store.wait()


def parts_of(table):
    parts, rest = [], np.asarray(table, np.float64)
    for _ in range(3):
        part = rest.astype(np.float32).astype(jnp.bfloat16)
        parts.append(part)
        rest = rest - part.astype(np.float64)
    return np.stack(parts)


def on_device(sizes, momenta, potential, rho_start, rho_end):
    A, G, B, T, X, Y = sizes
    piece, KT, pieces = X // A, NT // B, G * A
    stages = piece // ROWS
    assert Y == 128 and ROWS * T <= 128 and T % 8 == 0 and piece % ROWS == 0
    assert KT % 8 == 0 and pieces == (KT // 4) * B and ITERS > 1
    table_t, table_y = parts_of(cosine_table(NT)), parts_of(cosine_table(NY))
    turned_t, turned_y = parts_of(cosine_table(NT).T), parts_of(cosine_table(NY).T)
    e_t = eigenvalue(NT)
    spread_t = np.broadcast_to(e_t[:, None], (NT, 128)).astype(np.float32)
    spread_8 = np.broadcast_to(
        np.concatenate([e_t.reshape(NT // 4, 4)] * 2, axis=1)[:, :, None], (NT // 4, 8, 128)
    ).astype(np.float32)
    spread_y = np.broadcast_to(
        eigenvalue(NY).reshape(B, 1, 128), (B, 8, 128)
    ).astype(np.float32)
    tables = [
        table_t.reshape(3 * NT, NT), turned_t.reshape(3 * NT, NT), table_y, turned_y,
        spread_t, spread_8, spread_y,
    ]
    operands = [momenta, potential, rho_start, rho_end] + [
        jnp.asarray(np.ascontiguousarray(table)) for table in tables
    ]
    f32 = jnp.float32
    vmem = pl.BlockSpec(memory_space=pltpu.VMEM)
    hbm = pl.BlockSpec(memory_space=pl.ANY)
    dma = pltpu.SemaphoreType.DMA
    chunks = stages + 2

    def held(*shape, dtype=f32):
        return pltpu.VMEM(shape, dtype)

    return pl.pallas_call(
        functools.partial(kernel, sizes),
        out_shape=(
            jax.ShapeDtypeStruct(momenta.shape, f32),
            jax.ShapeDtypeStruct(potential.shape, f32),
        ),
        in_specs=[hbm, vmem, vmem, vmem, hbm, hbm, hbm, hbm, vmem, vmem, vmem],
        out_specs=(hbm, vmem),
        scratch_shapes=[
            held(3, T, X, Y),
            held(3, X, T, Y),
            held(3 * NT, NT, dtype=jnp.bfloat16),
            held(3 * NT, NT, dtype=jnp.bfloat16),
            held(3, NY, NY, dtype=jnp.bfloat16),
            held(3, NY, NY, dtype=jnp.bfloat16),
            held(ITERS + 1, X + 1, T, Y),
            held(ITERS, stages, A, 8, Y),
            held(ITERS, stages, 8, Y),
            held(ITERS, stages, A * ROWS, Y),
            held(ITERS, T, Y),
            held(ITERS, stages, 8, Y),
            held(ITERS, stages, 8, Y),
            held(stages, A * ROWS, Y),
            held(stages, 8, Y),
            held(stages, A, 8, Y),
            held(X, T, Y),
            held(A, piece, T, Y),
            held(ITERS, piece, NT, Y),
            held(piece, NT, Y),
            held(ITERS, piece, KT, NY),
            held(piece, KT, NY),
            held(piece, KT, NY),
            held(piece, KT, NY),
            held(ITERS, piece, NT, Y),
            held(piece, NT, Y),
            held(piece, KT, NY),
            held(piece, KT, NY),
            held(pieces, 8, 128),
            held(pieces, 8, 128),
            held(pieces, 8, 128),
            held(ITERS, pieces, 8, 128),
            held(pieces, 8, 128),
            held(ITERS, pieces, 8, 128),
            held(2, 8, 128),
            held(ITERS, pieces + 1, 8, 128),
            dma((5,)),
            dma((2,)),
            dma((2,)),
            dma((ITERS, stages)),
            dma((ITERS, stages)),
            dma((ITERS, stages, 2)),
            dma((ITERS, stages, 2)),
            dma((ITERS,)),
            dma((ITERS,)),
            dma((ITERS, stages, A - 1)),
            dma((ITERS, stages, A - 1)),
            dma((ITERS, A)),
            dma((ITERS,)),
            dma((ITERS, 2, chunks, A - 1)),
            dma((ITERS, 2, chunks, A - 1)),
            dma((ITERS, 2, chunks, B - 1)),
            dma((ITERS, 2, chunks, B - 1)),
            dma((ITERS, 2, pieces - 1)),
            dma((ITERS, 2, pieces - 1)),
            dma((ITERS, pieces)),
            dma((ITERS, pieces + 1)),
            dma((ITERS, 4, chunks)),
        ],
        compiler_params=pltpu.CompilerParams(
            collective_id=0, has_side_effects=True, vmem_limit_bytes=60 << 20
        ),
    )(*operands)


def solution(mesh):
    A, G, B = (mesh.shape[name] for name in ("ta", "gx", "gy"))
    sizes = (A, G, B, NT // A, NX // G, NY // B)
    placed = (P(None, "ta", "gx", "gy"), P("ta", "gx", "gy"), P("gx", "gy"), P("gx", "gy"))
    return jax.shard_map(
        functools.partial(on_device, sizes),
        mesh=mesh,
        in_specs=placed,
        out_specs=(P(None, "ta", "gx", "gy"), P("ta", "gx", "gy")),
        check_vma=False,
    )
```

```python
import functools

import jax
import jax.numpy as jnp
import numpy as np
from jax import lax
from jax.experimental import pallas as pl
from jax.experimental.pallas import tpu as pltpu
from jax.sharding import PartitionSpec as P

NT = 128
NX = 512
NY = 1024
ITERS = 2
NEWTON = 8
ROWS = 4
AHEAD = 4

MESH = pl.DeviceIdType.MESH


def cosine_table(count):
    modes = np.arange(count, dtype=np.int64)[:, None]
    cells = np.arange(count, dtype=np.int64)[None, :]
    phase = modes * (2 * cells + 1) % (4 * count)
    weight = np.where(modes == 0, 1.0, 2.0) / count
    return np.sqrt(weight) * np.cos(phase * (np.pi / (2 * count)))


def eigenvalue(count):
    return (2.0 * np.sin(np.arange(count) * (np.pi / (2 * count)))) ** 2


def split(value):
    parts = []
    for _ in range(3):
        part = value.astype(jnp.bfloat16)
        parts.append(part)
        value = value - part.astype(jnp.float32)
    return parts


def product(left, right):
    return jnp.dot(left, right, preferred_element_type=jnp.float32)


def table_right(value, table, kind):
    rows = value.shape[0]
    parts = split(value)
    total = product(parts[0], table[2, kind])
    middle_ = product(jnp.concatenate(parts[:2], axis=0), table[1, kind])
    large = product(jnp.concatenate(parts, axis=0), table[0, kind])
    total = total + (middle_[rows:] + large[2 * rows :])
    total = total + (middle_[:rows] + large[rows : 2 * rows])
    return total + large[:rows]


def table_left(table, value):
    rows = table.shape[0] // 3
    parts = split(value)
    first = product(table[: 2 * rows], jnp.concatenate(parts[:2], axis=0))
    second = product(table[2 * rows :], jnp.concatenate([parts[2], parts[0]], axis=0))
    return first[:rows] + (first[rows:] + second)


def turned(value):
    rows, lanes = value.shape
    index = 127 - lax.broadcasted_iota(jnp.int32, (rows, 128), 1)
    tiles = [
        jnp.take_along_axis(value[:, n * 128 : (n + 1) * 128], index, axis=1)
        for n in range(lanes // 128)
    ]
    return jnp.concatenate(tiles[::-1], axis=1)


def to_modes(value, table):
    half = value.shape[1] // 2
    left, right = value[:, :half], turned(value[:, half:])
    return jnp.concatenate(
        [table_right(left + right, table, 0), table_right(left - right, table, 1)], axis=1
    )


def from_modes(value, table):
    half = value.shape[1] // 2
    even = table_right(value[:, :half], table, 0)
    odd = table_right(value[:, half:], table, 1)
    return jnp.concatenate([even + odd, turned(even - odd)], axis=1)


def middle(ref, index):
    rows, group, lanes = ref.shape
    return ref.reshape(rows * group, lanes)[pl.ds(index, rows, stride=group), :]


def set_middle(ref, index, value):
    rows, group, lanes = ref.shape
    ref.reshape(rows * group, lanes)[pl.ds(index, rows, stride=group), :] = value


def project(p0, p1, p2):
    s = p1 * p1 + p2 * p2
    half = 0.5 * s
    lam = jnp.zeros_like(p0)
    for _ in range(NEWTON):
        growth = 1.0 + lam
        cube = growth * growth * growth
        lam = jnp.maximum(lam + ((p0 - lam) * cube + half * growth) / (cube + s), 0.0)
    inverse = 1.0 / (1.0 + lam)
    return p0 - lam, p1 * inverse, p2 * inverse


def kernel(
    sizes,
    mom_hbm, pot_in, rho_start, rho_end, ct_hbm, ctt_hbm, cy_hbm, cyt_hbm, et, et8, ey8,
    mom_out, pot_out,
    momv, momx, ct, ctt, cy, cyt,
    pot, ht, hyp, hwt, hwx, hwy, face_p, face_t, face_y, ht_out, wx_all, src,
    r1, s2, r2, sp, sq, s3, r3, s4, ci, cg, rip, rra,
    fwd_out, fwd_in, back_out, back_in, extra_out, extra_in,
    load_sem, halo_send, halo_recv, yh_send, yh_recv, w_send, w_recv, wx_send, wx_recv,
    th_send, th_recv, xh_send, xh_recv,
    t_send, t_recv, y_send, y_recv, p_send, p_recv, e_send, e_recv, local_sem,
):
    A, G, B, T, X, Y = sizes
    piece = X // A
    KT = NT // B
    pieces = G * A
    stages = piece // ROWS
    groups = X // ROWS
    high = ROWS * T
    ta, gx, gy = (lax.axis_index(name) for name in ("ta", "gx", "gy"))
    me = gx * A + ta
    to_t = [lax.rem(ta + d, A) for d in range(A)]
    to_x = [lax.rem(gx + d, G) for d in range(G)]
    to_y = [lax.rem(gy + d, B) for d in range(B)]
    partners = sorted(
        ((dx, dt) for dx in range(G) for dt in range(A) if dx or dt),
        key=lambda p: -(4 * (p[0] % 2) + min(p[0], G - p[0]) + min(p[1], A - p[1])),
    )

    def remote(source, target, send, recv, where):
        return pltpu.make_async_remote_copy(
            src_ref=source, dst_ref=target, send_sem=send, recv_sem=recv,
            device_id=where, device_id_type=MESH,
        )

    loads = [
        pltpu.make_async_copy(source, target, load_sem.at[n])
        for n, (source, target) in enumerate(
            ((mom_hbm, momv), (ct_hbm, ct), (cyt_hbm, cyt), (cy_hbm, cy), (ctt_hbm, ctt))
        )
    ]
    for load in loads:
        load.start()

    barrier = pltpu.get_barrier_semaphore()
    for dx, dt in partners:
        pl.semaphore_signal(
            barrier, inc=1, device_id=(to_t[dt], to_x[dx], gy), device_id_type=MESH
        )
    for d in range(1, B):
        pl.semaphore_signal(
            barrier, inc=1, device_id=(ta, gx, to_y[d]), device_id_type=MESH
        )

    sub = lax.broadcasted_iota(jnp.int32, (high, Y), 0)
    lane = lax.broadcasted_iota(jnp.int32, (high, Y), 1)
    eye = sub == lane
    time = lax.rem(sub, T)
    low = lax.broadcasted_iota(jnp.int32, (8, 128), 0) < 4

    def pack(column):
        spread = jnp.broadcast_to(column, (high, Y))
        return jnp.sum(jnp.where(eye, spread, 0.0), axis=0, keepdims=True)

    def unpack(row):
        spread = jnp.broadcast_to(row, (high, Y))
        return jnp.sum(jnp.where(eye, spread, 0.0), axis=1, keepdims=True)

    def rows_of(parts):
        return jnp.concatenate([jnp.broadcast_to(p, (T, Y)) for p in parts], axis=0)

    def pack_first(it, j):
        def group(a, _):
            x = (a * stages + j) * ROWS
            value = pot[it, pl.ds(x, ROWS), :, :].reshape(high, Y)
            face_p[it, j, pl.ds(a, 1), :] = pack(value[:, 0:1])
            return 0

        lax.fori_loop(0, A, group, 0)

    def first(a, _):
        for j in range(stages):
            for r in range(ROWS):
                x = (a * stages + j) * ROWS + r
                pot[0, x] = middle(pot_in, x)
                ht_out[j, a, r : r + 1, :] = pot_in[0, pl.ds(x, 1), :]
        return 0

    lax.fori_loop(0, A, first, 0)
    for j in range(stages):
        pack_first(0, j)
    pl.semaphore_wait(barrier, pieces + B - 2)

    def prepare():
        def coefficients(j, _):
            sigma = et[pl.ds(gy * KT, KT), :] + ey8[j][0:1, :]
            lanes = pl.ds(pl.multiple_of(j * 128, 128), 128)
            g = jnp.where(me == 0, 0.0, jnp.ones_like(sigma))
            h = sigma
            for i in range(piece - 1):
                inv = 1.0 / (g + 1.0 + h)
                g = g * inv
                ci[i, :, lanes] = inv
                cg[i, :, lanes] = g
                h = sigma + h * inv
            return 0

        lax.fori_loop(0, NY // 128, coefficients, 0)

        sigma = et8[gy * (KT // 4) + me // B] + ey8[lax.rem(me, B)]
        one = jnp.ones_like(sigma)

        def inner(i, state):
            g, h, h_first, ground = state
            inv = 1.0 / (g + 1.0 + h)
            inv_first = 1.0 / (1.0 + h_first)
            return (
                g * inv, sigma + h * inv, sigma + h_first * inv_first, ground + g * h * inv
            )

        link, h_end, h_first, ground = lax.fori_loop(
            0, piece - 1, inner, (one, sigma, sigma, jnp.zeros_like(sigma))
        )

        def outer(j, s):
            inv = 1.0 / (s + link)
            rip[j] = inv
            rra[j] = link * inv
            return jnp.where(j == pieces - 2, h_end, h_end + ground) + link * s * inv

        s_last = lax.fori_loop(0, pieces - 1, outer, h_first + ground)
        rip[pieces - 1] = jnp.where(
            s_last > 0.0, 1.0 / jnp.where(s_last > 0.0, s_last, 1.0), 0.0
        )

    def exchange(it, way, c, own, others, sends, recvs):
        local = pltpu.make_async_copy(*own, local_sem.at[it, way, c])
        local.start()
        copies = [
            remote(source, target, sends.at[it, way // 2, c, k], recvs.at[it, way // 2, c, k], where)
            for k, (source, target, where) in enumerate(others)
        ]
        for copy in copies:
            copy.start()
        return local, copies

    def along_t(it, way, c, source, target):
        return exchange(
            it, way, c, (source(ta), target),
            [(source(to_t[d]), target, (to_t[d], gx, gy)) for d in range(1, A)],
            t_send, t_recv,
        )

    def along_y(it, way, c, source, target):
        return exchange(
            it, way, c, (source(gy), target),
            [(source(to_y[d]), target, (ta, gx, to_y[d])) for d in range(1, B)],
            y_send, y_recv,
        )

    def landed(pair):
        pair[0].wait()
        for copy in pair[1]:
            copy.wait_recv()

    def sent(pairs):
        for pair in pairs:
            for copy in pair[1]:
                copy.wait_send()

    def place(i):
        return (i + piece - 1) % piece

    done = [ROWS * (j + 1) - 1 for j in range(stages)]
    cuts = [(j, ROWS * j - 1 if j else 0, done[j]) for j in range(stages - 1)]
    cuts += [(stages - 1, ROWS * (stages - 1) - 1, piece - 2), (stages - 1, piece - 2, piece)]
    marks = [0, 2] + list(range(5, piece, 3))[: 2 if stages > 2 else 0]
    marks += list(range(marks[-1] + ROWS, piece, ROWS)) + [piece]
    backs = list(zip(marks[:-1], marks[1:]))

    def y_face(it, j):
        return remote(
            face_p.at[it, j], hyp.at[it, j], yh_send.at[it, j], yh_recv.at[it, j],
            (ta, gx, to_y[B - 1]),
        )

    def t_face(it, j, d):
        return remote(
            ht_out.at[j, to_t[d]], ht.at[it + 1, j, ta], th_send.at[it, j, d - 1],
            th_recv.at[it, j, d - 1], (to_t[d], gx, gy),
        )

    def x_face(it, d):
        return remote(
            s4.at[0, pl.ds(d * T, T), :], pot.at[it + 1, X],
            xh_send.at[it, d], xh_recv.at[it], (d, to_x[G - 1], gy),
        )

    def wx_face(it):
        return remote(
            wx_all.at[X - 1], hwx.at[it], wx_send.at[it], wx_recv.at[it], (ta, to_x[1], gy)
        )

    halo = [
        remote(ht_out, ht.at[0], halo_send.at[0], halo_recv.at[0], (to_t[A - 1], gx, gy)),
        remote(pot.at[0, 0], pot.at[0, X], halo_send.at[1], halo_recv.at[1], (ta, to_x[G - 1], gy)),
    ]
    for j in range(stages):
        y_face(0, j).start()
    for copy in halo:
        copy.start()
    faces = [[] for _ in range(ITERS)]
    t_out = [[] for _ in range(ITERS)]
    unsent = []

    def project_rows(it, j):
        def group(a, _):
            n = a * stages + j
            x = n * ROWS
            here = pot[it, pl.ds(x, ROWS), :, :].reshape(high, Y)
            nxt = rows_of([ht[it, j, a, r : r + 1, :] for r in range(ROWS)])
            nxt = jnp.where(time == T - 1, nxt, pltpu.roll(here, high - 1, 0))
            edge_t = (time == T - 1) & (ta == A - 1)
            slope_t = jnp.where(edge_t, 0.0, nxt - here)
            nxt = pot[it, pl.ds(x + 1, ROWS), :, :].reshape(high, Y)
            edge_x = (sub >= high - T) & ((n == groups - 1) & (gx == G - 1))
            slope_x = jnp.where(edge_x, 0.0, nxt - here)
            nxt = jnp.where(
                lane == Y - 1, unpack(hyp[it, j, pl.ds(a, 1), :]), pltpu.roll(here, Y - 1, 1)
            )
            edge_y = (lane == Y - 1) & (gy == B - 1)
            slope_y = jnp.where(edge_y, 0.0, nxt - here)
            if it == 0:
                m = [
                    jnp.concatenate(
                        [middle(momv.at[b], x + r) for r in range(ROWS)], axis=0
                    )
                    for b in range(3)
                ]
            else:
                m = [momx[b, pl.ds(x, ROWS), :, :].reshape(high, Y) for b in range(3)]
            q = project(slope_t + m[0], slope_x + m[1], slope_y + m[2])
            m = [old + (s - new) for old, s, new in zip(m, (slope_t, slope_x, slope_y), q)]
            for b in range(3):
                if it == ITERS - 1:
                    for r in range(ROWS):
                        set_middle(momv.at[b], x + r, m[b][r * T : (r + 1) * T])
                else:
                    momx[b, pl.ds(x, ROWS), :, :] = m[b].reshape(ROWS, T, Y)
            wt = jnp.where(edge_t, 0.0, m[0] - q[0])
            wx = jnp.where(edge_x, 0.0, m[1] - q[1])
            wy = jnp.where(edge_y, 0.0, m[2] - q[2])
            for r in range(ROWS):
                face_t[j, pl.ds(a * ROWS + r, 1), :] = wt[(r + 1) * T - 1 : (r + 1) * T]
            face_y[j, pl.ds(a, 1), :] = pack(wy[:, Y - 1 : Y])
            wx_all[pl.ds(x, ROWS), :, :] = wx.reshape(ROWS, T, Y)
            last = rows_of([rho_end[pl.ds(x + r, 1), :] for r in range(ROWS)])
            begin = rows_of([rho_start[pl.ds(x + r, 1), :] for r in range(ROWS)])
            bound = jnp.where(edge_t, last, 0.0) - jnp.where(
                (time == 0) & (ta == 0), begin, 0.0
            )
            wt_back = jnp.where(time == 0, 0.0, pltpu.roll(wt, 1, 0))
            wy_back = jnp.where(lane == 0, 0.0, pltpu.roll(wy, 1, 1))
            value = wt - wt_back + wx + (wy - wy_back) + bound
            for r in range(ROWS):
                src[a, place(j * ROWS + r)] = value[r * T : (r + 1) * T]
            return 0

        lax.fori_loop(0, A, group, 0)

    def send_faces(it, j):
        copies = [
            remote(face_t.at[j], hwt.at[it, j], w_send.at[it, j, 0], w_recv.at[it, j, 0], (to_t[1], gx, gy)),
            remote(face_y.at[j], hwy.at[it, j], w_send.at[it, j, 1], w_recv.at[it, j, 1], (ta, gx, to_y[1])),
        ]
        for copy in copies:
            copy.start()
        return copies

    def finish_rows(it, j):
        def group(a, _):
            x = (a * stages + j) * ROWS
            before = unpack(hwy[it, j, pl.ds(a, 1), :])
            before = jnp.where((lane == 0) & (gy > 0), before, 0.0)
            early = rows_of([hwt[it, j, pl.ds(a * ROWS + r, 1), :] for r in range(ROWS)])
            before = before + jnp.where((time == 0) & (ta > 0), early, 0.0)
            for r in range(ROWS):
                value = src[a, place(j * ROWS + r)] - before[r * T : (r + 1) * T]
                if j + r:
                    value = value - wx_all[x + r - 1]
                src[a, place(j * ROWS + r)] = value
            return 0

        lax.fori_loop(0, A, group, 0)

    def close_stage(it, j):
        for copy in faces[it][j]:
            copy.wait_recv()
        finish_rows(it, j)
        if j == stages - 1:
            wx_face(it).wait_recv()
            src[0, place(0)] = src[0, place(0)] - jnp.where(gx > 0, hwx[it], 0.0)
            for a in range(1, A):
                src[a, place(0)] = src[a, place(0)] - wx_all[a * piece - 1]
        if j < AHEAD:
            send_chunk(it)

    def send_chunk(it):
        c = len(t_out[it])
        if c < len(cuts):
            _, lo, hi = cuts[c]
            t_out[it].append(
                along_t(
                    it, 0, c,
                    lambda other: src.at[other, pl.ds(lo, hi - lo), :, :],
                    r1.at[it, pl.ds(lo, hi - lo), pl.ds(ta * T, T), :],
                )
            )

    def run_stage(it, j):
        if it:
            for d in range(1, A):
                t_face(it - 1, j, d).wait_recv()
        y_face(it, j).wait_recv()
        if j == stages - 1:
            if it:
                x_face(it - 1, 0).wait_recv()
            else:
                halo[1].wait_recv()
        project_rows(it, j)
        faces[it].append(send_faces(it, j))
        if j == stages - 1:
            wx_face(it).start()
        if j:
            close_stage(it, j - 1)
        if j == stages - 1:
            close_stage(it, j)

    loads[0].wait()
    halo[0].wait_recv()
    for j in range(stages):
        run_stage(0, j)
    prepare()
    loads[1].wait()
    loads[2].wait()
    for copy in halo:
        copy.wait_send()

    for it in range(ITERS):
        if it == ITERS - 1:
            store = pltpu.make_async_copy(momv, mom_out, load_sem.at[0])
            store.start()

        y_out = []

        def forward_y(first_chunk, last_chunk):
            for c in range(first_chunk, last_chunk + 1):
                landed(y_out[c])
            lo, hi = cuts[first_chunk][1], cuts[last_chunk][2]
            value = r2[it, pl.ds(lo, hi - lo), :, :].reshape((hi - lo) * KT, NY)
            sp[pl.ds(lo, hi - lo)] = to_modes(value, cyt).reshape(hi - lo, KT, NY)

        for c, (_, lo, hi) in enumerate(cuts):
            landed(t_out[it][c])
            for a in range(lo, hi, 2):
                some = range(a, min(a + 2, hi))
                wide = jnp.concatenate([r1[it, p] for p in some], axis=1)
                wide = table_left(ct, wide)
                for n, p in enumerate(some):
                    s2[p] = wide[:, n * Y : (n + 1) * Y]
            y_out.append(
                along_y(
                    it, 1, c,
                    lambda other: s2.at[pl.ds(lo, hi - lo), pl.ds(other * KT, KT), :],
                    r2.at[it, pl.ds(lo, hi - lo), :, pl.ds(pl.multiple_of(gy * Y, Y), Y)],
                )
            )
            send_chunk(it)
            if c == 2:
                forward_y(0, 1)
            if c == 3:
                forward_y(2, 2)
        forward_y(3, len(cuts) - 1)

        def forward(j, _):
            lanes = pl.ds(pl.multiple_of(j * 128, 128), 128)
            value = sp[place(0), :, lanes]
            left = jnp.zeros_like(value)
            for i in range(piece - 1):
                left = left + cg[i, :, lanes] * value
                value = sp[place(i + 1), :, lanes] + ci[i, :, lanes] * value
                sp[place(i + 1), :, lanes] = value
            for q in range(KT // 4):
                part = slice(8 * (q // 2), 8 * (q // 2) + 8)
                a, b = left[part], value[part]
                if q % 2:
                    tile = jnp.where(low, pltpu.roll(a, 4, 0), b)
                else:
                    tile = jnp.where(low, a, pltpu.roll(b, 4, 0))
                fwd_out[q * B + j] = tile
            return 0

        inner_sum = jnp.zeros((8, 128), jnp.float32)
        for i in range(piece - 1):
            begin = 0.5 * (piece * (piece - 1) - i * (i + 1))
            other = 0.5 * (i + 1) * (piece - 1 - i)
            inner_sum = inner_sum + jnp.where(me == 0, begin, other) * sp[place(i), 0:8, 0:128]
        extra_out[0] = inner_sum
        lax.fori_loop(0, NY // 128, forward, 0)

        def scatter(phase, outgoing, incoming):
            copies = [
                remote(
                    outgoing.at[to_x[dx] * A + to_t[dt]], incoming.at[it, me],
                    p_send.at[it, phase, n], p_recv.at[it, phase, n],
                    (to_t[dt], to_x[dx], gy),
                )
                for n, (dx, dt) in enumerate(partners)
            ]
            for copy in copies:
                copy.start()
            incoming[it, me] = outgoing[me]
            return copies

        def gather_copy(k):
            return remote(
                extra_out.at[0], extra_in.at[it, k], e_send.at[it, k], e_recv.at[it, k],
                (0, 0, gy),
            )

        def spread_copy(k):
            return remote(
                extra_out.at[1], extra_in.at[it, pieces], e_send.at[it, k], e_recv.at[it, pieces],
                (lax.rem(k, A), k // A, gy),
            )

        head = (gy == 0) & (me == 0)
        tail = (gy == 0) & (me > 0)
        gathers = scatter(0, fwd_out, fwd_in)

        @pl.when(tail)
        def _():
            gather_copy(me).start()

        @pl.when(head)
        def _():
            extra_in[it, 0] = extra_out[0]

            @pl.loop(1, pieces)
            def _(k):
                gather_copy(k).wait_recv()

        for copy in gathers:
            copy.wait_recv()

        value = fwd_in[it, 0] + pltpu.roll(fwd_in[it, 1], 4, 0)
        before = [value]
        for j in range(1, pieces):
            given = fwd_in[it, j]
            if j + 1 < pieces:
                given = given + pltpu.roll(fwd_in[it, j + 1], 4, 0)
            value = given + rra[j - 1] * value
            before.append(value)
        full = value
        value = rip[pieces - 1] * value
        weighted = value * (0.5 * (piece + 1))
        for j in range(pieces - 2, -1, -1):
            here = rip[j] * before[j] + rra[j] * value
            back_out[j + 1] = jnp.where(low, pltpu.roll(here, 4, 0), value)
            value = here
            weighted = weighted + value * (
                piece + 0.5 * (piece - 1) if j == 0 else 1.0 * piece
            )
        back_out[0] = jnp.where(low, 0.0, value)
        returns = scatter(1, back_out, back_in)

        @pl.when(head)
        def _():
            total = lax.fori_loop(
                1, pieces, lambda k, acc: acc + extra_in[it, k], extra_in[it, 0]
            )
            excess = pltpu.roll(full, 4, 0)
            level = -(total + pltpu.roll(weighted, 4, 0)) / NX - excess * (
                (NX * NX - 1.0) / (6.0 * NX)
            )
            row = lax.broadcasted_iota(jnp.int32, (8, 128), 0)
            extra_out[1] = jnp.where(row == 0, excess, pltpu.roll(level, 1, 0))
            extra_in[it, pieces] = extra_out[1]

            @pl.loop(1, pieces)
            def _(k):
                spread_copy(k).start()

        if it == 0:
            loads[3].wait()
            loads[4].wait()
        for copy in returns:
            copy.wait_recv()

        @pl.when(tail)
        def _():
            spread_copy(me).wait_recv()

        def backward(j, _):
            lanes = pl.ds(pl.multiple_of(j * 128, 128), 128)
            left, value = [], []
            for n in range(KT // 8):
                a = back_in[it, 2 * n * B + j]
                b = back_in[it, (2 * n + 1) * B + j]
                left.append(jnp.where(low, a, pltpu.roll(b, 4, 0)))
                value.append(jnp.where(low, pltpu.roll(a, 4, 0), b))
            left = jnp.concatenate(left, axis=0)
            value = jnp.concatenate(value, axis=0)
            sq[piece - 1, :, lanes] = value
            for i in range(piece - 2, -1, -1):
                value = (
                    ci[i, :, lanes] * (sp[place(i), :, lanes] + value)
                    + cg[i, :, lanes] * left
                )
                sq[i, :, lanes] = value
            return 0

        lax.fori_loop(0, NY // 128, backward, 0)

        @pl.when(gy == 0)
        def _():
            row = lax.broadcasted_iota(jnp.int32, (8, 128), 0)
            constant = (row == 0) & (lax.broadcasted_iota(jnp.int32, (8, 128), 1) == 0)
            excess = extra_in[it, pieces]
            level = pltpu.roll(excess, 7, 0)
            for i in range(piece):
                cell = (me * piece + i).astype(jnp.float32)
                ramp = cell * (cell + 1.0) * (0.5 / NX)
                sq[i, 0:8, 0:128] += jnp.where(constant, excess * ramp + level, 0.0)

        y_back, t_back = [], []

        def backward_y(first_chunk, last_chunk):
            lo, hi = backs[first_chunk][0], backs[last_chunk][1]
            value = from_modes(sq[pl.ds(lo, hi - lo)].reshape((hi - lo) * KT, NY), cy)
            s3[pl.ds(lo, hi - lo)] = value.reshape(hi - lo, KT, NY)

        def send_lines():
            c = len(y_back)
            if c < len(backs):
                lines = pl.ds(backs[c][0], backs[c][1] - backs[c][0])
                y_back.append(
                    along_y(
                        it, 3, c,
                        lambda other: s3.at[
                            lines, :, pl.ds(pl.multiple_of(other * Y, Y), Y)
                        ],
                        r3.at[it, lines, pl.ds(gy * KT, KT), :],
                    )
                )

        backward_y(0, 0)
        send_lines()
        backward_y(1, 2)
        send_lines()
        more = it + 1 < ITERS
        sent(unsent)
        if it:

            @pl.when(ta == 0)
            def _():
                for d in range(A):
                    x_face(it - 1, d).wait_send()

        for c, (lo, hi) in enumerate(backs):
            landed(y_back[c])
            for x in range(lo, hi, 2):
                some = range(x, min(x + 2, hi))
                wide = jnp.concatenate([r3[it, p] for p in some], axis=1)
                wide = table_left(ctt, wide)
                for n, p in enumerate(some):
                    value = wide[:, n * Y : (n + 1) * Y]
                    s4[p] = value
                    if more:
                        for d in range(A):
                            t = (d + 1) * T % NT
                            r = p % ROWS
                            ht_out[p // ROWS, d, r : r + 1, :] = value[t : t + 1]
            if more:
                for j in range(stages):
                    if lo < ROWS * (j + 1) <= hi:
                        ht[it + 1, j, ta] = ht_out[j, ta]
                        for d in range(1, A):
                            t_face(it, j, d).start()
            t_back.append(
                along_t(
                    it, 2, c,
                    lambda other: s4.at[pl.ds(lo, hi - lo), pl.ds(other * T, T), :],
                    pot.at[it + 1, pl.ds(ta * piece + lo, hi - lo), pl.ds(0, T), :],
                )
            )
            send_lines()
            if c == 0:
                backward_y(3, len(backs) - 1)
            if more and c == 0:

                @pl.when(ta == 0)
                def _():
                    for d in range(A):
                        x_face(it, d).start()

        wx_face(it).wait_send()
        for j in range(stages):
            y_face(it, j).wait_send()
            for copy in faces[it][j]:
                copy.wait_send()
        sent(t_out[it] + y_out + y_back)
        for copy in gathers + returns:
            copy.wait_send()

        @pl.when(tail)
        def _():
            gather_copy(me).wait_send()

        @pl.when(head)
        def _():
            @pl.loop(1, pieces)
            def _(k):
                spread_copy(k).wait_send()

        for c, (lo, hi) in enumerate(backs):
            landed(t_back[c])
            for j in range(stages):
                if lo < ROWS * (j + 1) <= hi:
                    if more:
                        pack_first(it + 1, j)
                        y_face(it + 1, j).start()
                        if j:
                            run_stage(it + 1, j - 1)
                    else:

                        def arrived(a, _):
                            for r in range(ROWS):
                                x = (a * stages + j) * ROWS + r
                                set_middle(pot_out, x, pot[ITERS, x])
                            return 0

                        lax.fori_loop(0, A, arrived, 0)
        if more:
            run_stage(it + 1, stages - 1)
            for j in range(stages):
                for d in range(1, A):
                    t_face(it, j, d).wait_send()
        unsent = t_back
    sent(unsent)
    store.wait()


def parts_of(table):
    parts, rest = [], np.asarray(table, np.float64)
    for _ in range(3):
        part = rest.astype(np.float32).astype(jnp.bfloat16)
        parts.append(part)
        rest = rest - part.astype(np.float64)
    return np.stack(parts)


def stacked(table):
    h, m, l = parts_of(table)
    rows = [[h, h], [m, m], [h, l]]
    return np.concatenate([np.concatenate(row, axis=1) for row in rows], axis=0)


def on_device(sizes, momenta, potential, rho_start, rho_end):
    A, G, B, T, X, Y = sizes
    piece, KT, pieces = X // A, NT // B, G * A
    stages = piece // ROWS
    assert Y == 128 and ROWS * T <= 128 and T % 8 == 0 and piece % ROWS == 0
    assert stages == 4 and KT % 8 == 0 and pieces == (KT // 4) * B and ITERS > 1
    table_t = stacked(cosine_table(NT))
    turned_t = stacked(cosine_table(NT).T)
    folded = cosine_table(NY)[:, : NY // 2].reshape(NY // 2, 2, NY // 2).swapaxes(0, 1)
    table_y, turned_y = parts_of(folded), parts_of(folded.swapaxes(1, 2))
    e_y = eigenvalue(NY)
    e_y = np.concatenate([e_y[0::2], e_y[1::2]])
    e_t = eigenvalue(NT)
    spread_t = np.broadcast_to(e_t[:, None], (NT, 128)).astype(np.float32)
    spread_8 = np.broadcast_to(
        np.concatenate([e_t.reshape(NT // 4, 4)] * 2, axis=1)[:, :, None], (NT // 4, 8, 128)
    ).astype(np.float32)
    spread_y = np.broadcast_to(
        e_y.reshape(B, 1, 128), (B, 8, 128)
    ).astype(np.float32)
    tables = [
        table_t, turned_t, table_y, turned_y,
        spread_t, spread_8, spread_y,
    ]
    operands = [momenta, potential, rho_start, rho_end] + [
        jnp.asarray(np.ascontiguousarray(table)) for table in tables
    ]
    f32 = jnp.float32
    vmem = pl.BlockSpec(memory_space=pltpu.VMEM)
    hbm = pl.BlockSpec(memory_space=pl.ANY)
    dma = pltpu.SemaphoreType.DMA
    chunks = stages + 2

    def held(*shape, dtype=f32):
        return pltpu.VMEM(shape, dtype)

    return pl.pallas_call(
        functools.partial(kernel, sizes),
        out_shape=(
            jax.ShapeDtypeStruct(momenta.shape, f32),
            jax.ShapeDtypeStruct(potential.shape, f32),
        ),
        in_specs=[hbm, vmem, vmem, vmem, hbm, hbm, hbm, hbm, vmem, vmem, vmem],
        out_specs=(hbm, vmem),
        scratch_shapes=[
            held(3, T, X, Y),
            held(3, X, T, Y),
            held(3 * NT, 2 * NT, dtype=jnp.bfloat16),
            held(3 * NT, 2 * NT, dtype=jnp.bfloat16),
            held(3, 2, NY // 2, NY // 2, dtype=jnp.bfloat16),
            held(3, 2, NY // 2, NY // 2, dtype=jnp.bfloat16),
            held(ITERS + 1, X + 1, T, Y),
            held(ITERS, stages, A, 8, Y),
            held(ITERS, stages, 8, Y),
            held(ITERS, stages, A * ROWS, Y),
            held(ITERS, T, Y),
            held(ITERS, stages, 8, Y),
            held(ITERS, stages, 8, Y),
            held(stages, A * ROWS, Y),
            held(stages, 8, Y),
            held(stages, A, 8, Y),
            held(X, T, Y),
            held(A, piece, T, Y),
            held(ITERS, piece, NT, Y),
            held(piece, NT, Y),
            held(ITERS, piece, KT, NY),
            held(piece, KT, NY),
            held(piece, KT, NY),
            held(piece, KT, NY),
            held(ITERS, piece, NT, Y),
            held(piece, NT, Y),
            held(piece, KT, NY),
            held(piece, KT, NY),
            held(pieces, 8, 128),
            held(pieces, 8, 128),
            held(pieces, 8, 128),
            held(ITERS, pieces, 8, 128),
            held(pieces, 8, 128),
            held(ITERS, pieces, 8, 128),
            held(2, 8, 128),
            held(ITERS, pieces + 1, 8, 128),
            dma((5,)),
            dma((2,)),
            dma((2,)),
            dma((ITERS, stages)),
            dma((ITERS, stages)),
            dma((ITERS, stages, 2)),
            dma((ITERS, stages, 2)),
            dma((ITERS,)),
            dma((ITERS,)),
            dma((ITERS, stages, A - 1)),
            dma((ITERS, stages, A - 1)),
            dma((ITERS, A)),
            dma((ITERS,)),
            dma((ITERS, 2, chunks, A - 1)),
            dma((ITERS, 2, chunks, A - 1)),
            dma((ITERS, 2, chunks, B - 1)),
            dma((ITERS, 2, chunks, B - 1)),
            dma((ITERS, 2, pieces - 1)),
            dma((ITERS, 2, pieces - 1)),
            dma((ITERS, pieces)),
            dma((ITERS, pieces + 1)),
            dma((ITERS, 4, chunks)),
        ],
        compiler_params=pltpu.CompilerParams(
            collective_id=0, has_side_effects=True, vmem_limit_bytes=60 << 20
        ),
    )(*operands)


def solution(mesh):
    A, G, B = (mesh.shape[name] for name in ("ta", "gx", "gy"))
    sizes = (A, G, B, NT // A, NX // G, NY // B)
    placed = (P(None, "ta", "gx", "gy"), P("ta", "gx", "gy"), P("gx", "gy"), P("gx", "gy"))
    return jax.shard_map(
        functools.partial(on_device, sizes),
        mesh=mesh,
        in_specs=placed,
        out_specs=(P(None, "ta", "gx", "gy"), P("ta", "gx", "gy")),
        check_vma=False,
    )
```
